512 devices in a mesh: ctx: 128 (over z, y, x_hi), head: 4 (over x_lo, core).
Axes of the slice: x: 4 (x_hi: 2, x_lo: 2; x = x_hi * 2 + x_lo), y: 4, z: 16, core: 2. Of those that a mesh axis runs over, the one named last changes fastest.
Arguments:
- query_rows: bfloat16 [2, 8192, 3072], P(None, 'ctx', 'head'), may hold values from -4 to 4
- key_rows: bfloat16 [2, 8192, 3072], P(None, 'ctx', 'head'), may hold values from -4 to 4
- value_rows: bfloat16 [2, 8192, 3072], P(None, 'ctx', 'head'), may hold values from -4 to 4
- out_grad: bfloat16 [2, 8192, 3072], P(None, 'ctx', 'head'), may hold values from -16 to 16
- log_norms: float32 [2, 2, 12, 8192], P(None, None, 'head', 'ctx'), may hold values from 3 to 4.5
- row_deltas: float32 [2, 2, 12, 8192], P(None, None, 'head', 'ctx'), may hold values from -16 to 16
- lambdas: float32 [12], P('head'), may hold values from 0.3 to 0.9
Outputs:
- query_grad: bfloat16 [2, 8192, 3072], P(None, ('ctx', 'head'))
- key_grad: bfloat16 [2, 8192, 3072], P(None, ('ctx', 'head'))
- value_grad: bfloat16 [2, 8192, 3072], P(None, ('ctx', 'head'))
- lambda_grad: float32 [12], P('head')
The draws below stay inside these ranges and needn't reach their ends.
All inputs are finite; a program needn't handle non-finite values.
Results may differ from the reference program's by a relative error of at most 0.039.
Values may be sent and summed in bfloat16 or wider, within the bound.
A program may use at most 64 MiB of HBM per device.

```python
import math
import jax
import jax.numpy as jnp
from jax import lax

HEADS = 12
DK = 128
DV = 256
BLK = 64
CYCLE = 3
BLOCKS = 128
HALF = 8192


def draw_out_grad(key, part):
    key = jax.random.fold_in(key, 7)
    rising = 1.0 + 2.0 * jnp.arange(HALF, dtype=jnp.float32) / HALF
    shape = (2, HALF, HEADS * DV)
    base = jnp.clip(jax.random.normal(key, shape, jnp.float32), -4.0, 4.0)
    return (base * rising[None, :, None]).astype(jnp.bfloat16)


def level_of(rng, dims, pieces, smallest, largest):
    loudness, own = 1.0, jax.random.fold_in(rng, 6)
    for axis_at, shards_of in pieces:
        steps = jnp.exp(jax.random.uniform(jax.random.fold_in(own, axis_at), (shards_of,), jnp.float32, smallest / len(pieces), largest / len(pieces)))
        loudness = loudness * jnp.repeat(steps, dims[axis_at] // shards_of).reshape([-1 if axis == axis_at else 1 for axis in range(len(dims))])
    return loudness


def gaussian(stream_key, dims, scale, bound, cuts=(), kind=jnp.bfloat16):
    gain = level_of(stream_key, dims, cuts, -0.22, 0.18) if cuts else 1.0
    result = jax.random.normal(stream_key, dims, jnp.float32) * scale * gain
    return jnp.minimum(jnp.maximum(result, -bound), bound).astype(kind)


def setup_inputs(seed: int = 0) -> dict:
    key_of = jax.random.split(jax.random.key(seed), 8)
    query_rows = gaussian(key_of[0], (2, HALF, HEADS * 2 * DK), 1.0, 4.0, ((1, 128), (2, 4)))
    key_rows = gaussian(key_of[1], (2, HALF, HEADS * 2 * DK), 1.0, 4.0, ((1, 128), (2, 4)))
    value_rows = gaussian(key_of[2], (2, HALF, HEADS * DV), 1.0, 4.0, ((1, 128), (2, 4)))
    out_grad = draw_out_grad(jax.random.fold_in(key_of[7], 71), 0)
    log_norms = jnp.clip(3.0 + 1.5 * jax.random.uniform(key_of[4], (2, 2, HEADS, HALF), jnp.float32) ** level_of(key_of[4], (2, 2, HEADS, HALF), ((2, 4), (3, 128)), -0.2, 0.2), 3.0, 4.5)
    row_deltas = gaussian(key_of[5], (2, 2, HEADS, HALF), 4.0, 16.0, ((2, 4), (3, 128)), jnp.float32)
    lambdas = jnp.clip(0.3 + 0.59999996 * jax.random.uniform(key_of[6], (HEADS,), jnp.float32) ** level_of(key_of[6], (HEADS,), ((0, 4),), -0.2, 0.2), 0.3, 0.9)
    return dict(query_rows=query_rows, key_rows=key_rows, value_rows=value_rows, out_grad=out_grad, log_norms=log_norms, row_deltas=row_deltas, lambdas=lambdas)


def tile_grads(query_tile, key_tile, value_tile, grad_tile, norm_tile, delta_tile, lambdas, allowed):
    single = jnp.float32
    score_scale = 1.0 / math.sqrt(query_tile.shape[-1])
    scores = jnp.einsum('qhmc,khmc->hmqk', query_tile.astype(single), key_tile.astype(single)) * score_scale
    attn_probs = jnp.where(allowed[None, None], jnp.exp(scores - jnp.swapaxes(norm_tile, 0, 1)[:, :, :, None]), 0.0)
    grad_inner = jnp.einsum('qhc,khc->hqk', grad_tile.astype(single), value_tile.astype(single))
    mixed_probs = (attn_probs[:, 0] - lambdas[:, None, None] * attn_probs[:, 1]).astype(jnp.bfloat16)
    value_grad = jnp.einsum('hqk,qhc->khc', mixed_probs.astype(single), grad_tile.astype(single))
    factor = jnp.stack([jnp.ones_like(lambdas), -lambdas], axis=1)[:, :, None, None]
    shifted = grad_inner[:, None] - jnp.swapaxes(delta_tile, 0, 1)[:, :, :, None]
    score_grad = (score_scale * factor * attn_probs * shifted).astype(jnp.bfloat16)
    query_grad = jnp.einsum('hmqk,khmc->qhmc', score_grad.astype(single), key_tile.astype(single))
    key_grad = jnp.einsum('hmqk,qhmc->khmc', score_grad.astype(single), query_tile.astype(single))
    lambda_part = -lax.optimization_barrier(jnp.sum(attn_probs[:, 1] * grad_inner, axis=(1, 2)))
    return (query_grad, key_grad, value_grad, lambda_part)

def positions(half_index, owner, seq_len):
    start = jnp.where(half_index == 0, owner * BLK, seq_len - BLK * (owner + 1))
    return (start + jnp.arange(BLK, dtype=jnp.int32)).astype(jnp.int32)

def reference(query_rows, key_rows, value_rows, out_grad, log_norms, row_deltas, lambdas):
    block_count = BLOCKS
    seq_len = 2 * block_count * BLK
    query_six = query_rows.reshape(2, block_count, BLK, HEADS, 2, DK)
    key_six = key_rows.reshape(2, block_count, BLK, HEADS, 2, DK)
    value_five = value_rows.reshape(2, block_count, BLK, HEADS, DV)
    grad_five = out_grad.reshape(2, block_count, BLK, HEADS, DV)
    norm_five = log_norms.reshape(2, 2, HEADS, block_count, BLK)
    delta_five = row_deltas.reshape(2, 2, HEADS, block_count, BLK)

    def visit(visit_step):

        def one_owner(k_owner):
            q_owner = ((k_owner - visit_step) % block_count).astype(jnp.int32)
            query_parts = [jnp.zeros((BLK, HEADS, 2, DK), jnp.float32), jnp.zeros((BLK, HEADS, 2, DK), jnp.float32)]
            key_parts = [jnp.zeros((BLK, HEADS, 2, DK), jnp.float32), jnp.zeros((BLK, HEADS, 2, DK), jnp.float32)]
            value_parts = [jnp.zeros((BLK, HEADS, DV), jnp.float32), jnp.zeros((BLK, HEADS, DV), jnp.float32)]
            lambda_total = jnp.zeros((HEADS,), jnp.float32)
            for query_half in range(2):
                for key_half in range(2):
                    allowed = positions(key_half, k_owner, seq_len)[None, :] <= positions(query_half, q_owner, seq_len)[:, None]
                    tile_terms = tile_grads(query_six[query_half, q_owner], key_six[key_half, k_owner], value_five[key_half, k_owner], grad_five[query_half, q_owner], norm_five[query_half, :, :, q_owner], delta_five[query_half, :, :, q_owner], lambdas, allowed)
                    query_parts[query_half] = query_parts[query_half] + tile_terms[0]
                    key_parts[key_half] = key_parts[key_half] + tile_terms[1]
                    value_parts[key_half] = value_parts[key_half] + tile_terms[2]
                    lambda_total = lambda_total + tile_terms[3]
            return (jnp.stack(query_parts), jnp.stack(key_parts), jnp.stack(value_parts), lambda_total)
        return lax.map(one_owner, jnp.arange(block_count, dtype=jnp.int32))
    query_total = jnp.zeros((block_count, 2, BLK, HEADS, 2, DK), jnp.float32)
    key_total = jnp.zeros((block_count, 2, BLK, HEADS, 2, DK), jnp.float32)
    value_total = jnp.zeros((block_count, 2, BLK, HEADS, DV), jnp.float32)
    lambda_grad = jnp.zeros((HEADS,), jnp.float32)
    for visit_step in range(CYCLE):
        q_part, k_part, v_part, l_part = visit(visit_step)
        query_total = query_total + jnp.roll(q_part, -visit_step, axis=0)
        key_total = key_total + k_part
        value_total = value_total + v_part
        lambda_grad = lambda_grad + lax.optimization_barrier(jnp.sum(l_part, axis=0))
    query_grad = jnp.transpose(query_total, (1, 0, 2, 3, 4, 5)).reshape(2, block_count * BLK, HEADS * 2 * DK).astype(jnp.bfloat16)
    key_grad = jnp.transpose(key_total, (1, 0, 2, 3, 4, 5)).reshape(2, block_count * BLK, HEADS * 2 * DK).astype(jnp.bfloat16)
    value_grad = jnp.transpose(value_total, (1, 0, 2, 3, 4)).reshape(2, block_count * BLK, HEADS * DV).astype(jnp.bfloat16)
    return (query_grad, key_grad, value_grad, lambda_grad)
```

```python
import functools
import math

import jax
import jax.numpy as jnp
from jax import lax
from jax.experimental import pallas as pl
from jax.experimental.pallas import tpu as pltpu
from jax.sharding import PartitionSpec as P

MESH = pl.DeviceIdType.MESH
F32, BF16 = jnp.float32, jnp.bfloat16
HG = 3
BLK = 64
NH = 4
ROWS = BLK // NH
W = 256
SCALE = 1.0 / math.sqrt(128.0)


def nt(a, b):
    return lax.dot_general(a, b, (((1,), (1,)), ((), ())), preferred_element_type=F32)


def nn(a, b):
    return lax.dot_general(a, b, (((1,), (0,)), ((), ())), preferred_element_type=F32)


def tn(a, b):
    return lax.dot_general(a, b, (((0,), (0,)), ((), ())), preferred_element_type=F32)


def tile_pass(q, do, k, v, rows, lam, mask):
    n0, n1, d0, d1 = rows
    s0 = nt(k[:, :128], q[:, :128])
    s1 = nt(k[:, 128:], q[:, 128:])
    inner = nt(v, do)
    p0 = jnp.where(mask, jnp.exp(s0 * SCALE - n0), 0.0)
    p1 = jnp.where(mask, jnp.exp(s1 * SCALE - n1), 0.0)
    mixed = (p0 - lam * p1).astype(BF16)
    g0 = (SCALE * p0 * (inner - d0)).astype(BF16)
    g1 = ((-lam * SCALE) * p1 * (inner - d1)).astype(BF16)
    dv = nn(mixed, do)
    dk = jnp.concatenate([nn(g0, q[:, :128]), nn(g1, q[:, 128:])], axis=1)
    dq = jnp.concatenate([tn(g0, k[:, :128]), tn(g1, k[:, 128:])], axis=1)
    lam_row = jnp.sum(p1 * inner, axis=0, keepdims=True)
    return dq, dk, dv, lam_row


def kernel(
    n,
    q_hbm, k_hbm, v_hbm, do_hbm, norm_hbm, delta_hbm, lam_ref,
    oq_hbm, ok_hbm, ov_hbm, lam_out,
    q_v, k_v, v_v, do_v, nv, dv_, nd, ndr, rnd, rbuf, wbuf,
    acc_k, acc_v, st_q, st_k, st_v, st_p, st_w, pq, pw, fin_q, lam_tile, lbuf1, lbuf2,
    in_sem, out_sem, qs_send, q_recv, nd_send, nd_recv, ws_send, w_recv,
    r_send, r_recv, p_send, p_recv, pw_send, pw_recv, l_send, l_recv,
):
    me = lax.axis_index("ctx")
    hd = lax.axis_index("head")
    z, r8 = me // 8, me % 8

    def ctx(d):
        return lax.rem(me + (d + n), n)

    def head(d):
        return lax.rem(hd + d, NH)

    loads = [
        pltpu.make_async_copy(a, b, in_sem.at[i])
        for i, (a, b) in enumerate(
            [(q_hbm, q_v), (do_hbm, do_v), (norm_hbm, nv), (delta_hbm, dv_), (k_hbm, k_v), (v_hbm, v_v)]
        )
    ]
    for c in loads:
        c.start()

    barrier = pltpu.get_barrier_semaphore()

    def tell(c, h):
        pl.semaphore_signal(barrier, inc=1, device_id=(c, h), device_id_type=MESH)

    for s in (1, 2):
        tell(ctx(-s), hd)
        for d in range(NH):
            tell(ctx(s), head(d))
    for d in range(1, NH):
        tell(me, head(d))
    for d in range(1, 8):
        tell(z * 8 + lax.rem(r8 + d, 8), hd)
    for d in range(1, 16):
        tell(lax.rem(z + d, 16) * 8 + r8, hd)
    pl.semaphore_wait(barrier, 10 + 3 + 7 + 15)

    loads[0].wait()
    loads[1].wait()
    for g in range(HG):
        cols = pl.ds(g * W, W)
        for s in (1, 2):
            for a, src in enumerate((q_v, do_v)):
                pltpu.make_async_remote_copy(
                    src_ref=src.at[1, :, cols], dst_ref=rbuf.at[g, a, s - 1],
                    send_sem=qs_send.at[s - 1, a], recv_sem=q_recv.at[g],
                    device_id=(ctx(s), hd), device_id_type=MESH,
                ).start()
        if g == 0:
            loads[2].wait()
            loads[3].wait()
            for half in range(2):
                for m in range(2):
                    nd[3 * m : 3 * m + 3, half * 64 : half * 64 + 64] = nv[half, m]
                    nd[8 + 3 * m : 11 + 3 * m, half * 64 : half * 64 + 64] = dv_[half, m]
            for s in (1, 2):
                pltpu.make_async_remote_copy(
                    src_ref=nd, dst_ref=rnd.at[s - 1],
                    send_sem=nd_send.at[s - 1], recv_sem=nd_recv,
                    device_id=(ctx(s), hd), device_id_type=MESH,
                ).start()
    for s in (1, 2):

        @pl.when(me + s >= n)
        def _():
            for g in range(HG):
                for a, src in enumerate((q_v, do_v)):
                    pltpu.make_async_remote_copy(
                        src_ref=src.at[0, :, pl.ds(g * W, W)], dst_ref=wbuf.at[g, a, s - 1],
                        send_sem=ws_send.at[s - 1, a], recv_sem=w_recv.at[s - 1, g],
                        device_id=(ctx(s), hd), device_id_type=MESH,
                    ).start()

    @pl.when(me == 1)
    def _():
        for g in range(HG):
            for a in range(2):
                wbuf[g, a, 0] = jnp.zeros((BLK, W), BF16)

    loads[4].wait()
    loads[5].wait()

    kk = lax.broadcasted_iota(jnp.int32, (128, 128), 0)
    qq = lax.broadcasted_iota(jnp.int32, (128, 128), 1)
    own_mask = ((kk < 64) & (qq >= 64)) | (((kk < 64) == (qq < 64)) & (kk <= qq))
    lim = jnp.where(qq < 64, 1, 2)
    rem_mask = (kk < 64) | (me >= lim)
    wrap_mask = (kk < 64) & (me < lim)

    def rows_of(ref, g):
        return [ref[i : i + 1, :] for i in (g, 3 + g, 8 + g, 11 + g)]

    def kv_of(g):
        cols = pl.ds(g * W, W)
        return k_v[:, :, cols].reshape(128, W), v_v[:, :, cols].reshape(128, W)

    def out_cols(g):
        return pl.ds(pl.multiple_of((hd * HG + g) * W, W), W)

    def rows_at(h):
        return pl.ds(pl.multiple_of(h * ROWS, ROWS), ROWS)

    def spread(stage, dst, g, i):
        for d in range(1, NH):
            pltpu.make_async_remote_copy(
                src_ref=stage.at[g, :, rows_at(head(d)), :], dst_ref=dst.at[:, :, out_cols(g)],
                send_sem=r_send.at[i, g], recv_sem=r_recv.at[i],
                device_id=(me, head(d)), device_id_type=MESH,
            ).start()
        pltpu.make_async_copy(
            stage.at[g, :, rows_at(hd), :], dst.at[:, :, out_cols(g)], out_sem.at[i]
        ).start()

    lam_tile[...] = jnp.zeros((8, 128), F32)
    for g in range(HG):
        cols = pl.ds(g * W, W)
        k, v = kv_of(g)
        q = q_v[:, :, cols].reshape(128, W)
        do = do_v[:, :, cols].reshape(128, W)
        dq, dk, dv, lam_row = tile_pass(q, do, k, v, rows_of(nd, g), lam_ref[g], own_mask)
        st_q[g] = dq.astype(BF16).reshape(2, BLK, W)
        acc_k[g] = dk
        acc_v[g] = dv
        lam_tile[g : g + 1, :] = lam_row
        spread(st_q, pq.at[pl.ds(0, 2)], g, 0)

    def wait_for(ref, sem):
        pltpu.make_async_copy(ref, ref, sem).wait()

    wait_for(rnd, nd_recv)
    left = lax.broadcasted_iota(jnp.int32, (16, 128), 1) < 64
    ndr[0] = jnp.where(left, pltpu.roll(rnd[0], 64, 1), rnd[1])

    @pl.when(me < 2)
    def _():
        ndr[1] = jnp.where(left, rnd[0], pltpu.roll(rnd[1], 64, 1))

    for g in range(HG):
        wait_for(rbuf.at[g], q_recv.at[g])

        for s in (1, 2):

            @pl.when(me < s)
            def _():
                wait_for(wbuf.at[g, :, s - 1], w_recv.at[s - 1, g])

        @pl.when(me < 2)
        def _():
            k, v = kv_of(g)
            dq, dk, dv, lam_row = tile_pass(
                wbuf[g, 0].reshape(128, W), wbuf[g, 1].reshape(128, W), k, v,
                rows_of(ndr.at[1], g), lam_ref[g], wrap_mask,
            )
            st_w[g] = dq.astype(BF16).reshape(2, BLK, W)
            acc_k[g] += dk
            acc_v[g] += dv
            lam_tile[g : g + 1, :] += lam_row

        for s in (1, 2):

            @pl.when(me < s)
            def _():
                for d in range(NH):
                    pltpu.make_async_remote_copy(
                        src_ref=st_w.at[g, s - 1, rows_at(head(d)), :],
                        dst_ref=pw.at[s - 1, :, out_cols(g)],
                        send_sem=pw_send.at[s - 1, g], recv_sem=pw_recv.at[s - 1],
                        device_id=(ctx(-s), head(d)), device_id_type=MESH,
                    ).start()

        k, v = kv_of(g)
        dq, dk, dv, lam_row = tile_pass(
            rbuf[g, 0].reshape(128, W), rbuf[g, 1].reshape(128, W), k, v,
            rows_of(ndr.at[0], g), lam_ref[g], rem_mask,
        )
        st_p[g] = dq.astype(BF16).reshape(2, BLK, W)
        st_k[g] = (acc_k[g] + dk).astype(BF16).reshape(2, BLK, W)
        st_v[g] = (acc_v[g] + dv).astype(BF16).reshape(2, BLK, W)
        lam_tile[g : g + 1, :] += lam_row
        spread(st_k, ok_hbm, g, 1)
        spread(st_v, ov_hbm, g, 2)
        for s in (1, 2):
            for d in range(NH):
                pltpu.make_async_remote_copy(
                    src_ref=st_p.at[g, s - 1, rows_at(head(d)), :],
                    dst_ref=pq.at[s + 1, :, out_cols(g)],
                    send_sem=p_send.at[s - 1, g], recv_sem=p_recv,
                    device_id=(ctx(-s), head(d)), device_id_type=MESH,
                ).start()

    lbuf1[r8] = lam_tile[...]
    for d in range(1, 8):
        pltpu.make_async_remote_copy(
            src_ref=lam_tile, dst_ref=lbuf1.at[r8],
            send_sem=l_send.at[0], recv_sem=l_recv.at[0],
            device_id=(z * 8 + lax.rem(r8 + d, 8), hd), device_id_type=MESH,
        ).start()
    wait_for(lbuf1.at[pl.ds(0, 7)], l_recv.at[0])
    wait_for(lbuf1.at[pl.ds(0, 7)], l_send.at[0])
    total = lbuf1[0]
    for i in range(1, 8):
        total = total + lbuf1[i]
    lam_tile[...] = total
    lbuf2[z] = total
    for d in range(1, 16):
        pltpu.make_async_remote_copy(
            src_ref=lam_tile, dst_ref=lbuf2.at[z],
            send_sem=l_send.at[1], recv_sem=l_recv.at[1],
            device_id=(lax.rem(z + d, 16) * 8 + r8, hd), device_id_type=MESH,
        ).start()
    wait_for(lbuf2.at[pl.ds(0, 15)], l_recv.at[1])
    wait_for(lbuf2.at[pl.ds(0, 15)], l_send.at[1])
    total = lbuf2[0]
    for i in range(1, 16):
        total = total + lbuf2[i]
    lam_out[...] = jnp.broadcast_to(-jnp.sum(total, axis=1, keepdims=True), (8, 128))

    part = pl.ds(0, 3 * HG * W)
    wait_for(pq.at[pl.ds(0, 2), :, part], r_recv.at[0])
    for g in range(HG):
        wait_for(st_q.at[g, :, pl.ds(0, ROWS)], out_sem.at[0])
    wait_for(pq.at[pl.ds(2, 2)], p_recv)
    for s in (1, 2):

        @pl.when(me + s >= n)
        def _():
            wait_for(pw.at[s - 1], pw_recv.at[s - 1])

    fin_q[0] = pq[0]
    fin_q[1] = (pq[1].astype(F32) + pq[2].astype(F32) + pq[3].astype(F32)).astype(BF16)

    @pl.when(me == n - 1)
    def _():
        fin_q[0] = (pq[0].astype(F32) + pw[0].astype(F32) + pw[1].astype(F32)).astype(BF16)

    @pl.when(me == n - 2)
    def _():
        fin_q[0] = (pq[0].astype(F32) + pw[1].astype(F32)).astype(BF16)

    last = pltpu.make_async_copy(fin_q, oq_hbm, out_sem.at[3])
    last.start()

    wait_for(ok_hbm.at[:, :, part], r_recv.at[1])
    wait_for(ov_hbm.at[:, :, part], r_recv.at[2])
    for g in range(HG):
        wait_for(st_k.at[g, :, pl.ds(0, ROWS)], out_sem.at[1])
        wait_for(st_v.at[g, :, pl.ds(0, ROWS)], out_sem.at[2])

    for s in (1, 2):
        for a, src in enumerate((q_v, do_v)):
            wait_for(src.at[1], qs_send.at[s - 1, a])
        wait_for(nd, nd_send.at[s - 1])
        for g in range(HG):
            wait_for(st_p.at[g, s - 1], p_send.at[s - 1, g])

        @pl.when(me + s >= n)
        def _():
            for a, src in enumerate((q_v, do_v)):
                wait_for(src.at[0], ws_send.at[s - 1, a])

        @pl.when(me < s)
        def _():
            for g in range(HG):
                wait_for(st_w.at[g, s - 1], pw_send.at[s - 1, g])

    for i, stage in enumerate((st_q, st_k, st_v)):
        for g in range(HG):
            wait_for(stage.at[g, :, pl.ds(0, 3 * ROWS)], r_send.at[i, g])
    last.wait()


def local(query_rows, key_rows, value_rows, out_grad, log_norms, row_deltas, lambdas):
    n = lax.axis_size("ctx")
    hbm = pl.BlockSpec(memory_space=pl.ANY)
    half = (2, BLK, HG * W)
    out = jax.ShapeDtypeStruct((2, ROWS, NH * HG * W), BF16)
    dma = pltpu.SemaphoreType.DMA
    oq, ok, ov, lam = pl.pallas_call(
        functools.partial(kernel, n),
        out_shape=(out, out, out, jax.ShapeDtypeStruct((8, 128), F32)),
        in_specs=[hbm] * 6 + [pl.BlockSpec(memory_space=pltpu.SMEM)],
        out_specs=(hbm, hbm, hbm, pl.BlockSpec(memory_space=pltpu.VMEM)),
        scratch_shapes=[
            pltpu.VMEM(half, BF16), pltpu.VMEM(half, BF16), pltpu.VMEM(half, BF16), pltpu.VMEM(half, BF16),
            pltpu.VMEM((2, 2, HG, BLK), F32), pltpu.VMEM((2, 2, HG, BLK), F32),
            pltpu.VMEM((16, 128), F32), pltpu.VMEM((2, 16, 128), F32), pltpu.VMEM((2, 16, 128), F32),
            pltpu.VMEM((HG, 2, 2, BLK, W), BF16), pltpu.VMEM((HG, 2, 2, BLK, W), BF16),
            pltpu.VMEM((HG, 2 * BLK, W), F32), pltpu.VMEM((HG, 2 * BLK, W), F32),
            pltpu.VMEM((HG, 2, BLK, W), BF16), pltpu.VMEM((HG, 2, BLK, W), BF16),
            pltpu.VMEM((HG, 2, BLK, W), BF16), pltpu.VMEM((HG, 2, BLK, W), BF16),
            pltpu.VMEM((HG, 2, BLK, W), BF16),
            pltpu.VMEM((4, ROWS, NH * HG * W), BF16), pltpu.VMEM((2, ROWS, NH * HG * W), BF16),
            pltpu.VMEM((2, ROWS, NH * HG * W), BF16),
            pltpu.VMEM((8, 128), F32), pltpu.VMEM((8, 8, 128), F32), pltpu.VMEM((16, 8, 128), F32),
            dma((6,)), dma((4,)), dma((2, 2)), dma((HG,)), dma((2,)), dma, dma((2, 2)), dma((2, HG)),
            dma((3, HG)), dma((3,)), dma((2, HG)), dma, dma((2, HG)), dma((2,)), dma((2,)), dma((2,)),
        ],
        compiler_params=pltpu.CompilerParams(
            collective_id=0, has_side_effects=True, vmem_limit_bytes=32 * 1024 * 1024
        ),
        cost_estimate=pl.CostEstimate(flops=3 * 10**8, bytes_accessed=2 * 10**6, transcendentals=2 * 10**5),
        name="diff_attention_backward",
    )(query_rows, key_rows, value_rows, out_grad, log_norms, row_deltas, lambdas)
    return oq, ok, ov, lam[:HG, 0]


def solution(mesh):
    in_specs = (
        P(None, "ctx", "head"),
        P(None, "ctx", "head"),
        P(None, "ctx", "head"),
        P(None, "ctx", "head"),
        P(None, None, "head", "ctx"),
        P(None, None, "head", "ctx"),
        P("head"),
    )
    out_specs = (
        P(None, ("ctx", "head"), None),
        P(None, ("ctx", "head"), None),
        P(None, ("ctx", "head"), None),
        P("head"),
    )
    return jax.shard_map(local, mesh=mesh, in_specs=in_specs, out_specs=out_specs, check_vma=False)
```

```python
import functools
import math

import jax
import jax.numpy as jnp
from jax import lax
from jax.experimental import pallas as pl
from jax.experimental.pallas import tpu as pltpu
from jax.sharding import PartitionSpec as P

MESH = pl.DeviceIdType.MESH
F32, BF16 = jnp.float32, jnp.bfloat16
HG = 3
BLK = 64
NH = 4
ROWS = BLK // NH
W = 256
COLS = NH * HG * W
PLANE = 8
DEPTH = 16
SCALE = 1.0 / math.sqrt(128.0)


def nt(a, b):
    return lax.dot_general(a, b, (((1,), (1,)), ((), ())), preferred_element_type=F32)


def nn(a, b):
    return lax.dot_general(a, b, (((1,), (0,)), ((), ())), preferred_element_type=F32)


def tn(a, b):
    return lax.dot_general(a, b, (((0,), (0,)), ((), ())), preferred_element_type=F32)


def tile_pass(q, do, k, v, rows, lam, mask):
    n0, n1, d0, d1 = rows
    s0 = nt(k[:, :128], q[:, :128])
    s1 = nt(k[:, 128:], q[:, 128:])
    inner = nt(v, do)
    p0 = jnp.where(mask, jnp.exp(s0 * SCALE - n0), 0.0)
    p1 = jnp.where(mask, jnp.exp(s1 * SCALE - n1), 0.0)
    mixed = (p0 - lam * p1).astype(BF16)
    g0 = (SCALE * p0 * (inner - d0)).astype(BF16)
    g1 = ((-lam * SCALE) * p1 * (inner - d1)).astype(BF16)
    dv = nn(mixed, do)
    dk = jnp.concatenate([nn(g0, q[:, :128]), nn(g1, q[:, 128:])], axis=1)
    dq = jnp.concatenate([tn(g0, k[:, :128]), tn(g1, k[:, 128:])], axis=1)
    lam_row = jnp.sum(p1 * inner, axis=0, keepdims=True)
    return dq, dk, dv, lam_row


def wait_for(ref, sem):
    pltpu.make_async_copy(ref, ref, sem).wait()


def rounded(x):
    return x.astype(BF16).reshape(2, BLK, W)


def main_kernel(
    n,
    q_hbm, k_hbm, v_hbm, do_hbm, norm_hbm, delta_hbm, lam_hbm,
    pq, lk, lv, lbuf2,
    lam_s, q_v, k_v, v_v, do_v, nv, dv_, nd, ndr, rnd, rbuf, wbuf,
    acc_q, acc_k, acc_v, st_q, st_k, st_v, st_p, st_wk, st_wv, wk, wv, lam_tile, lbuf1,
    in_sem, out_sem, qs_send, q_recv, nd_send, nd_recv, ws_send, w_recv,
    r_send, r_recv, p_send, p_recv, pw_send, pw_recv, l_send, l_recv, line_sem,
):
    me = lax.axis_index("ctx")
    hd = lax.axis_index("head")
    z, r8 = me // PLANE, me % PLANE

    def ctx(d):
        return lax.rem(me + (d + n), n)

    def head(d):
        return lax.rem(hd + d, NH)

    def line(d):
        return lax.rem(z + d, DEPTH) * PLANE + r8

    def ahead(s):
        return me + s < n

    def behind(s):
        return me >= s

    loads = [
        pltpu.make_async_copy(a, b, in_sem.at[i])
        for i, (a, b) in enumerate(
            [(q_hbm, q_v), (do_hbm, do_v), (norm_hbm, nv), (delta_hbm, dv_), (k_hbm, k_v), (v_hbm, v_v), (lam_hbm, lam_s)]
        )
    ]
    for c in loads:
        c.start()

    barrier = pltpu.get_barrier_semaphore()

    def tell(c, h):
        pl.semaphore_signal(barrier, inc=1, device_id=(c, h), device_id_type=MESH)

    for s in (1, 2):
        for d in range(NH):
            tell(ctx(s), head(d))
            tell(ctx(-s), head(d))
    for d in range(1, NH):
        tell(me, head(d))
    for d in range(1, PLANE):
        tell(z * PLANE + lax.rem(r8 + d, PLANE), hd)

    @pl.when(z == 0)
    def _():
        for d in range(1, DEPTH):
            tell(line(d), hd)

    pl.semaphore_wait(barrier, 4 * NH + (NH - 1) + (PLANE - 1) + jnp.where(z > 0, 1, 0))

    @pl.when(z > 0)
    def _():
        pl.semaphore_signal(line_sem.at[0], inc=1, device_id=(r8, hd), device_id_type=MESH)

    loads[0].wait()
    loads[1].wait()
    for g in range(HG):
        cols = pl.ds(g * W, W)
        for s in (1, 2):

            @pl.when(ahead(s))
            def _():
                for a, src in enumerate((q_v, do_v)):
                    pltpu.make_async_remote_copy(
                        src_ref=src.at[1, :, cols], dst_ref=rbuf.at[g, a, s - 1],
                        send_sem=qs_send.at[s - 1, a], recv_sem=q_recv.at[s - 1, g],
                        device_id=(ctx(s), hd), device_id_type=MESH,
                    ).start()
                pass

        if g == 0:
            loads[2].wait()
            loads[3].wait()
            for half in range(2):
                lanes = pl.ds(half * BLK, BLK)
                for i in range(HG):
                    nd[2 * i : 2 * i + 2, lanes] = nv[half, i]
                    nd[8 + 2 * i : 10 + 2 * i, lanes] = dv_[half, i]
            for s in (1, 2):

                @pl.when(ahead(s))
                def _():
                    pltpu.make_async_remote_copy(
                        src_ref=nd, dst_ref=rnd.at[s - 1],
                        send_sem=nd_send.at[s - 1], recv_sem=nd_recv.at[s - 1],
                        device_id=(ctx(s), hd), device_id_type=MESH,
                    ).start()
                    pass

            for c in loads[4:]:
                c.wait()
        for s in (1, 2):

            @pl.when(~behind(s))
            def _():
                for a, src in enumerate((k_v, v_v)):
                    pltpu.make_async_remote_copy(
                        src_ref=src.at[0, :, cols], dst_ref=wbuf.at[g, a, s - 1],
                        send_sem=ws_send.at[s - 1, a], recv_sem=w_recv.at[s - 1, g],
                        device_id=(ctx(-s), hd), device_id_type=MESH,
                    ).start()
                rbuf[g, :, s - 1] = jnp.zeros((2, BLK, W), BF16)
                if g == 0:
                    rnd[s - 1] = jnp.zeros((16, 128), F32)

    @pl.when(me == n - 2)
    def _():
        wbuf[:, :, 0] = jnp.zeros((HG, 2, BLK, W), BF16)

    for s in (1, 2):

        @pl.when(~ahead(s))
        def _():
            pq[s + 1] = jnp.zeros((ROWS, COLS), BF16)

    kk = lax.broadcasted_iota(jnp.int32, (128, 128), 0)
    qq = lax.broadcasted_iota(jnp.int32, (128, 128), 1)
    own_mask = ((kk < 64) & (qq >= 64)) | (((kk < 64) == (qq < 64)) & (kk <= qq))
    rem_mask = (kk < 64) | (qq < 64) | (me >= 2)
    rem_mask = rem_mask & (me >= jnp.where(qq < 64, 1, 2))
    wrap_mask = (kk >= 64) | (me >= n - 1)

    def rows_of(ref, g):
        return [ref[i : i + 1, :] for i in (2 * g, 2 * g + 1, 8 + 2 * g, 9 + 2 * g)]

    def own(ref, g):
        return ref[:, :, pl.ds(g * W, W)].reshape(2 * BLK, W)

    def out_cols(g):
        return pl.ds(pl.multiple_of((hd * HG + g) * W, W), W)

    def rows_at(h):
        return pl.ds(pl.multiple_of(h * ROWS, ROWS), ROWS)

    def spread(stage, dst, g, i):
        for d in range(1, NH):
            pltpu.make_async_remote_copy(
                src_ref=stage.at[g, :, rows_at(head(d)), :], dst_ref=dst.at[:, :, out_cols(g)],
                send_sem=r_send.at[i, g], recv_sem=r_recv.at[i],
                device_id=(me, head(d)), device_id_type=MESH,
            ).start()
        pltpu.make_async_copy(
            stage.at[g, :, rows_at(hd), :], dst.at[:, :, out_cols(g)], out_sem.at[i]
        ).start()

    def give_back(stage, dst, g, c, send, recv):
        for d in range(NH):
            pltpu.make_async_remote_copy(
                src_ref=stage.at[rows_at(head(d)), :], dst_ref=dst.at[:, out_cols(g)],
                send_sem=send, recv_sem=recv,
                device_id=(c, head(d)), device_id_type=MESH,
            ).start()

    own_q = pq.at[pl.ds(0, 2)]
    last_two = me >= n - 2
    lam_tile[...] = jnp.zeros((8, 128), F32)
    for g in range(HG):
        dq, dk, dv, lam_row = tile_pass(
            own(q_v, g), own(do_v, g), own(k_v, g), own(v_v, g), rows_of(nd, g), lam_s[g], own_mask
        )
        st_q[g] = rounded(dq)
        acc_q[g] = dq
        acc_k[g] = dk
        acc_v[g] = dv
        lam_tile[g : g + 1, :] = lam_row

        @pl.when(~last_two)
        def _():
            spread(st_q, own_q, g, 0)

    @pl.when(z == 0)
    def _():
        pl.semaphore_wait(line_sem.at[0], DEPTH - 1)
        for d in range(1, DEPTH):
            pl.semaphore_signal(line_sem.at[1], inc=1, device_id=(line(d), hd), device_id_type=MESH)

    for s in (1, 2):

        @pl.when(behind(s))
        def _():
            wait_for(rnd.at[s - 1], nd_recv.at[s - 1])

    left = lax.broadcasted_iota(jnp.int32, (16, 128), 1) < BLK
    ndr[...] = jnp.where(left, pltpu.roll(rnd[0], BLK, 1), rnd[1])

    for g in range(HG):
        for s in (1, 2):

            @pl.when(behind(s))
            def _():
                wait_for(rbuf.at[g, :, s - 1], q_recv.at[s - 1, g])

        dq, dk, dv, lam_row = tile_pass(
            rbuf[g, 0].reshape(2 * BLK, W), rbuf[g, 1].reshape(2 * BLK, W), own(k_v, g), own(v_v, g),
            rows_of(ndr, g), lam_s[g], rem_mask,
        )
        st_p[g] = rounded(dq)
        st_k[g] = rounded(acc_k[g] + dk)
        st_v[g] = rounded(acc_v[g] + dv)
        lam_tile[g : g + 1, :] += lam_row
        spread(st_k, lk, g, 1)
        spread(st_v, lv, g, 2)
        for s in (1, 2):

            @pl.when(behind(s))
            def _():
                give_back(st_p.at[g, s - 1], pq.at[s + 1], g, ctx(-s), p_send.at[s - 1, g], p_recv.at[s - 1])

        @pl.when(last_two)
        def _():
            for s in (1, 2):

                @pl.when(~ahead(s))
                def _():
                    wait_for(wbuf.at[g, :, s - 1], w_recv.at[s - 1, g])

            dq, dk, dv, lam_row = tile_pass(
                own(q_v, g), own(do_v, g), wbuf[g, 0].reshape(2 * BLK, W), wbuf[g, 1].reshape(2 * BLK, W),
                rows_of(nd, g), lam_s[g], wrap_mask,
            )
            st_q[g] = rounded(acc_q[g] + dq)
            st_wk[g] = rounded(dk)
            st_wv[g] = rounded(dv)
            lam_tile[g : g + 1, :] += lam_row
            for s in (1, 2):

                @pl.when(~ahead(s))
                def _():
                    give_back(st_wk.at[g, s - 1], wk.at[s - 1], g, ctx(s), pw_send.at[s - 1, g, 0], pw_recv.at[s - 1, 0])
                    give_back(st_wv.at[g, s - 1], wv.at[s - 1], g, ctx(s), pw_send.at[s - 1, g, 1], pw_recv.at[s - 1, 1])

            spread(st_q, own_q, g, 0)

    lbuf1[r8] = lam_tile[...]
    for d in range(1, PLANE):
        pltpu.make_async_remote_copy(
            src_ref=lbuf1.at[r8], dst_ref=lbuf1.at[r8],
            send_sem=l_send.at[0], recv_sem=l_recv.at[0],
            device_id=(z * PLANE + lax.rem(r8 + d, PLANE), hd), device_id_type=MESH,
        ).start()

    @pl.when(z > 0)
    def _():
        pl.semaphore_wait(line_sem.at[1], 1)

    wait_for(lbuf1.at[pl.ds(0, PLANE - 1)], l_recv.at[0])
    total = lbuf1[0]
    for i in range(1, PLANE):
        total = total + lbuf1[i]
    lbuf2[z] = total
    for d in range(1, DEPTH):
        pltpu.make_async_remote_copy(
            src_ref=lbuf2.at[z], dst_ref=lbuf2.at[z],
            send_sem=l_send.at[1], recv_sem=l_recv.at[1],
            device_id=(line(d), hd), device_id_type=MESH,
        ).start()

    part = pl.ds(0, (NH - 1) * HG * W)
    for i, (dst, stage) in enumerate(((own_q, st_q), (lk, st_k), (lv, st_v))):
        wait_for(dst.at[:, :, part], r_recv.at[i])
        for g in range(HG):
            wait_for(stage.at[g, :, pl.ds(0, ROWS)], out_sem.at[i])
    for s in (1, 2):

        @pl.when(ahead(s))
        def _():
            wait_for(pq.at[s + 1], p_recv.at[s - 1])

        @pl.when(~behind(s))
        def _():
            for i, (dst, term) in enumerate(((lk, wk), (lv, wv))):
                wait_for(term.at[s - 1], pw_recv.at[s - 1, i])

    @pl.when(me == 0)
    def _():
        for dst, term in ((lk, wk), (lv, wv)):
            dst[0] = (dst[0].astype(F32) + term[0].astype(F32) + term[1].astype(F32)).astype(BF16)

    @pl.when(me == 1)
    def _():
        for dst, term in ((lk, wk), (lv, wv)):
            dst[0] = (dst[0].astype(F32) + term[1].astype(F32)).astype(BF16)


    for s in (1, 2):

        @pl.when(ahead(s))
        def _():
            for a, src in enumerate((q_v, do_v)):
                wait_for(src.at[1], qs_send.at[s - 1, a])
            wait_for(nd, nd_send.at[s - 1])
            pass

        @pl.when(~behind(s))
        def _():
            for a, src in enumerate((k_v, v_v)):
                wait_for(src.at[0], ws_send.at[s - 1, a])
            pass

        for g in range(HG):

            @pl.when(behind(s))
            def _():
                wait_for(st_p.at[g, s - 1], p_send.at[s - 1, g])

            @pl.when(~ahead(s))
            def _():
                wait_for(st_wk.at[g, s - 1], pw_send.at[s - 1, g, 0])
                wait_for(st_wv.at[g, s - 1], pw_send.at[s - 1, g, 1])

    for i, stage in enumerate((st_q, st_k, st_v)):
        for g in range(HG):
            wait_for(stage.at[g, :, pl.ds(0, (NH - 1) * ROWS)], r_send.at[i, g])
    wait_for(lbuf1.at[pl.ds(0, PLANE - 1)], l_send.at[0])
    wait_for(lbuf2.at[pl.ds(0, DEPTH - 1)], l_recv.at[1])
    wait_for(lbuf2.at[pl.ds(0, DEPTH - 1)], l_send.at[1])


def finish_kernel(pq, lk, lv, lbuf2, oq, ok, ov, lam_out, sum_q, sems):
    copies = [
        pltpu.make_async_copy(lk, ok, sems.at[0]),
        pltpu.make_async_copy(lv, ov, sems.at[1]),
        pltpu.make_async_copy(pq.at[0], oq.at[0], sems.at[2]),
        pltpu.make_async_copy(sum_q, oq.at[1], sems.at[3]),
    ]
    for c in copies[:3]:
        c.start()
    sum_q[...] = (pq[1].astype(F32) + pq[2].astype(F32) + pq[3].astype(F32)).astype(BF16)
    copies[3].start()
    total = lbuf2[0]
    for i in range(1, DEPTH):
        total = total + lbuf2[i]
    for g in range(HG):
        lam_out[g] = -jnp.sum(total[g : g + 1, :])
    for c in copies:
        c.wait()


def local(query_rows, key_rows, value_rows, out_grad, log_norms, row_deltas, lambdas):
    n = lax.axis_size("ctx")
    hbm = pl.BlockSpec(memory_space=pl.ANY)
    vmem = pl.BlockSpec(memory_space=pltpu.VMEM)
    smem = pl.BlockSpec(memory_space=pltpu.SMEM)
    half = (2, BLK, HG * W)
    tile = (HG, 2, BLK, W)
    dma, regular = pltpu.SemaphoreType.DMA, pltpu.SemaphoreType.REGULAR
    args = (
        query_rows, key_rows, value_rows, out_grad,
        jnp.swapaxes(log_norms, 1, 2), jnp.swapaxes(row_deltas, 1, 2), lambdas,
    )
    pq, lk, lv, sums = pl.pallas_call(
        functools.partial(main_kernel, n),
        out_shape=(
            pltpu.VMEM((4, ROWS, COLS), BF16),
            pltpu.VMEM((2, ROWS, COLS), BF16), pltpu.VMEM((2, ROWS, COLS), BF16),
            pltpu.VMEM((DEPTH, 8, 128), F32),
        ),
        in_specs=[hbm] * 7,
        out_specs=(vmem,) * 4,
        scratch_shapes=[
            pltpu.SMEM((HG,), F32),
            pltpu.VMEM(half, BF16), pltpu.VMEM(half, BF16), pltpu.VMEM(half, BF16), pltpu.VMEM(half, BF16),
            pltpu.VMEM((2, HG, 2, BLK), F32), pltpu.VMEM((2, HG, 2, BLK), F32),
            pltpu.VMEM((16, 128), F32), pltpu.VMEM((16, 128), F32), pltpu.VMEM((2, 16, 128), F32),
            pltpu.VMEM((HG, 2, 2, BLK, W), BF16), pltpu.VMEM((HG, 2, 2, BLK, W), BF16),
            *[pltpu.VMEM((HG, 2 * BLK, W), F32) for _ in range(3)],
            *[pltpu.VMEM(tile, BF16) for _ in range(6)],
            pltpu.VMEM((2, ROWS, COLS), BF16), pltpu.VMEM((2, ROWS, COLS), BF16),
            pltpu.VMEM((8, 128), F32), pltpu.VMEM((PLANE, 8, 128), F32),
            dma((7,)), dma((3,)), dma((2, 2)), dma((2, HG)), dma((2,)), dma((2,)), dma((2, 2)), dma((2, HG)),
            dma((3, HG)), dma((3,)), dma((2, HG)), dma((2,)), dma((2, HG, 2)), dma((2, 2)), dma((2,)), dma((2,)),
            regular((2,)),
        ],
        compiler_params=pltpu.CompilerParams(
            collective_id=0, has_side_effects=True, vmem_limit_bytes=24 * 1024 * 1024
        ),
        cost_estimate=pl.CostEstimate(flops=3 * 10**8, bytes_accessed=2 * 10**6, transcendentals=2 * 10**5),
        name="attention_backward",
    )(*[pltpu.with_memory_space_constraint(x, pltpu.HBM) for x in args])
    out = jax.ShapeDtypeStruct((2, ROWS, COLS), BF16)
    return pl.pallas_call(
        finish_kernel,
        out_shape=(out, out, out, jax.ShapeDtypeStruct((HG,), F32)),
        in_specs=[vmem] * 4,
        out_specs=(hbm, hbm, hbm, smem),
        scratch_shapes=[pltpu.VMEM((ROWS, COLS), BF16), dma((4,))],
        compiler_params=pltpu.CompilerParams(vmem_limit_bytes=16 * 1024 * 1024),
        name="write_outputs",
    )(*[pltpu.with_memory_space_constraint(x, pltpu.VMEM) for x in (pq, lk, lv, sums)])


def solution(mesh):
    in_specs = (
        P(None, "ctx", "head"),
        P(None, "ctx", "head"),
        P(None, "ctx", "head"),
        P(None, "ctx", "head"),
        P(None, None, "head", "ctx"),
        P(None, None, "head", "ctx"),
        P("head"),
    )
    out_specs = (
        P(None, ("ctx", "head"), None),
        P(None, ("ctx", "head"), None),
        P(None, ("ctx", "head"), None),
        P("head"),
    )
    return jax.shard_map(local, mesh=mesh, in_specs=in_specs, out_specs=out_specs, check_vma=False)
```

```python
import functools
import math

import jax
import jax.numpy as jnp
from jax import lax
from jax.experimental import pallas as pl
from jax.experimental.pallas import tpu as pltpu
from jax.sharding import PartitionSpec as P

MESH = pl.DeviceIdType.MESH
F32, BF16 = jnp.float32, jnp.bfloat16
HG = 3
BLK = 64
NH = 4
ROWS = BLK // NH
W = 256
COLS = NH * HG * W
PLANE = 8
DEPTH = 16
SCALE = 1.0 / math.sqrt(128.0)


def nt(a, b):
    return lax.dot_general(a, b, (((1,), (1,)), ((), ())), preferred_element_type=F32)


def nn(a, b):
    return lax.dot_general(a, b, (((1,), (0,)), ((), ())), preferred_element_type=F32)


def tn(a, b):
    return lax.dot_general(a, b, (((0,), (0,)), ((), ())), preferred_element_type=F32)


def second_map(q1, do, k1, v, rows, mask):
    inner = nt(v, do)
    p1 = jnp.where(mask, jnp.exp(nt(k1, q1) * SCALE - rows[1]), 0.0)
    return p1, inner, jnp.sum(p1 * inner, axis=0, keepdims=True)


def gradients(p1, inner, q0, q1, do, k0, k1, rows, lam, mask):
    n0, _, d0, d1 = rows
    p0 = jnp.where(mask, jnp.exp(nt(k0, q0) * SCALE - n0), 0.0)
    mixed = (p0 - lam * p1).astype(BF16)
    g0 = (SCALE * p0 * (inner - d0)).astype(BF16)
    g1 = ((-lam * SCALE) * p1 * (inner - d1)).astype(BF16)
    dv = nn(mixed, do)
    dk = jnp.concatenate([nn(g0, q0), nn(g1, q1)], axis=1)
    dq = jnp.concatenate([tn(g0, k0), tn(g1, k1)], axis=1)
    return dq, dk, dv


def wait_for(ref, sem):
    pltpu.make_async_copy(ref, ref, sem).wait()


def rounded(x):
    return x.astype(BF16).reshape(2, BLK, W)


def main_kernel(
    n,
    q_hbm, k_hbm, v_hbm, do_hbm, norm_hbm, delta_hbm, lam_hbm,
    pq, lk, lv, lbuf2,
    lam_s, q_v, k_v, v_v, do_v, nv, dv_, nd, ndr, rnd, r_a, r_b, w_a, w_b, h_a, h_b, h_nd,
    r_p1, r_in, w_p1, w_in,
    acc_k, acc_v, st_q, st_k, st_v, st_p, st_wk, st_wv, st_wq, wk, wv, wq, lam_tile, lbuf1,
    in_sem, out_sem, qs_send, a_recv, b_recv, nd_send, nd_recv, ws_send, wa_recv, wb_recv,
    hs_send, ha_recv, hb_recv, hn_recv, wq_send, wq_recv,
    r_send, r_recv, p_send, p_recv, pw_send, pw_recv, l_send, l_recv, line_sem,
):
    me = lax.axis_index("ctx")
    hd = lax.axis_index("head")
    z, r8 = me // PLANE, me % PLANE

    def ctx(d):
        return lax.rem(me + (d + n), n)

    def head(d):
        return lax.rem(hd + d, NH)

    def line(d):
        return lax.rem(z + d, DEPTH) * PLANE + r8

    def ahead(s):
        return me + s < n

    def behind(s):
        return me >= s

    last_two = me >= n - 2
    host = (me >= PLANE - 2) & (me < PLANE)
    guest = me + (n - PLANE)

    def hosts(s):
        return host & (me + s >= PLANE)

    loads = [
        pltpu.make_async_copy(a, b, in_sem.at[i])
        for i, (a, b) in enumerate(
            [(q_hbm, q_v), (do_hbm, do_v), (norm_hbm, nv), (delta_hbm, dv_), (k_hbm, k_v), (v_hbm, v_v), (lam_hbm, lam_s)]
        )
    ]
    for c in loads:
        c.start()

    barrier = pltpu.get_barrier_semaphore()

    def tell(c, h):
        pl.semaphore_signal(barrier, inc=1, device_id=(c, h), device_id_type=MESH)

    heads = range(NH)
    for s in (1, 2):

        @pl.when(ahead(s))
        def _():
            for d in heads:
                tell(ctx(s), head(d))

        @pl.when(behind(s))
        def _():
            for d in heads:
                tell(ctx(-s), head(d))

        @pl.when(~behind(s))
        def _():
            for d in heads:
                tell(me - s + PLANE, head(d))

    for d in range(1, NH):
        tell(me, head(d))
    for d in range(1, PLANE):
        tell(z * PLANE + lax.rem(r8 + d, PLANE), hd)

    @pl.when(z == 0)
    def _():
        for d in range(1, DEPTH):
            tell(line(d), hd)

    @pl.when(host)
    def _():
        for d in range(1, NH):
            tell(guest, head(d))

    def when(condition, count):
        return jnp.where(condition, count, 0)

    pl.semaphore_wait(
        barrier,
        sum(when(ahead(s), NH) + when(behind(s), NH) + when(hosts(s), NH) for s in (1, 2))
        + when(z > 0, 1) + when(last_two, NH - 1) + (NH - 1) + (PLANE - 1),
    )

    @pl.when(z > 0)
    def _():
        pl.semaphore_signal(line_sem.at[0], inc=1, device_id=(r8, hd), device_id_type=MESH)

    @pl.when(last_two)
    def _():
        for d in heads:
            pl.semaphore_signal(line_sem.at[2], inc=1, device_id=(r8, head(d)), device_id_type=MESH)

    def map_cols(g, m):
        return pl.ds(g * W + m * 128, 128)

    def send_first(src, wide, half, dst, g, s, c, send, recv):
        for i, (ref, cols, lanes) in enumerate(
            ((src, map_cols(g, 1), pl.ds(0, 128)), (wide, pl.ds(g * W, W), pl.ds(128, W)))
        ):
            pltpu.make_async_remote_copy(
                src_ref=ref.at[half, :, cols], dst_ref=dst.at[g, s - 1, :, lanes],
                send_sem=send.at[s - 1, i], recv_sem=recv.at[s - 1, g],
                device_id=(c, hd), device_id_type=MESH,
            ).start()

    def send_second(src, half, dst, g, s, c, send, recv):
        pltpu.make_async_remote_copy(
            src_ref=src.at[half, :, map_cols(g, 0)], dst_ref=dst.at[g, s - 1],
            send_sem=send.at[s - 1, 2], recv_sem=recv.at[s - 1, g],
            device_id=(c, hd), device_id_type=MESH,
        ).start()

    loads[0].wait()
    loads[1].wait()

    @pl.when(last_two)
    def _():
        for g in range(HG):
            for i, (ref, cols, lanes) in enumerate(
                ((q_v, map_cols(g, 1), pl.ds(0, 128)), (do_v, pl.ds(g * W, W), pl.ds(128, W)))
            ):
                pltpu.make_async_remote_copy(
                    src_ref=ref.at[:, :, cols], dst_ref=h_a.at[g, :, :, lanes],
                    send_sem=hs_send.at[i], recv_sem=ha_recv.at[g],
                    device_id=(r8, hd), device_id_type=MESH,
                ).start()

    for g in range(HG):
        for s in (1, 2):

            @pl.when(ahead(s))
            def _():
                send_first(q_v, do_v, 1, r_a, g, s, ctx(s), qs_send, a_recv)

    for c in loads[2:]:
        c.wait()
    for half in range(2):
        lanes = pl.ds(half * BLK, BLK)
        for i in range(HG):
            nd[2 * i : 2 * i + 2, lanes] = nv[half, i]
            nd[8 + 2 * i : 10 + 2 * i, lanes] = dv_[half, i]
    for s in (1, 2):

        @pl.when(ahead(s))
        def _():
            pltpu.make_async_remote_copy(
                src_ref=nd, dst_ref=rnd.at[s - 1],
                send_sem=nd_send.at[s - 1], recv_sem=nd_recv.at[s - 1],
                device_id=(ctx(s), hd), device_id_type=MESH,
            ).start()

        @pl.when(~behind(s))
        def _():
            for g in range(HG):
                send_first(k_v, v_v, 0, w_a, g, s, me - s + PLANE, ws_send, wa_recv)

    @pl.when(last_two)
    def _():
        pltpu.make_async_remote_copy(
            src_ref=nd, dst_ref=h_nd, send_sem=hs_send.at[2], recv_sem=hn_recv,
            device_id=(r8, hd), device_id_type=MESH,
        ).start()
        for g in range(HG):
            pltpu.make_async_remote_copy(
                src_ref=q_v.at[:, :, map_cols(g, 0)], dst_ref=h_b.at[g],
                send_sem=hs_send.at[3], recv_sem=hb_recv.at[g],
                device_id=(r8, hd), device_id_type=MESH,
            ).start()

    for s in (1, 2):

        @pl.when(ahead(s))
        def _():
            for g in range(HG):
                send_second(q_v, 1, r_b, g, s, ctx(s), qs_send, b_recv)

        @pl.when(~behind(s))
        def _():
            for g in range(HG):
                send_second(k_v, 0, w_b, g, s, me - s + PLANE, ws_send, wb_recv)


    for s in (1, 2):

        @pl.when(~behind(s))
        def _():
            r_a[:, s - 1] = jnp.zeros((HG, BLK, 128 + W), BF16)
            r_b[:, s - 1] = jnp.zeros((HG, BLK, 128), BF16)
            rnd[s - 1] = jnp.zeros((16, 128), F32)

    @pl.when(me == PLANE - 2)
    def _():
        w_a[:, 0] = jnp.zeros((HG, BLK, 128 + W), BF16)
        w_b[:, 0] = jnp.zeros((HG, BLK, 128), BF16)

    @pl.when(me == n - 1)
    def _():
        pq[2] = jnp.zeros((ROWS, COLS), BF16)

    kk = lax.broadcasted_iota(jnp.int32, (128, 128), 0)
    qq = lax.broadcasted_iota(jnp.int32, (128, 128), 1)
    own_mask = ((kk < 64) & (qq >= 64)) | (((kk < 64) == (qq < 64)) & (kk <= qq))
    rem_mask = (kk < 64) | (qq < 64) | (me >= 2)
    rem_mask = rem_mask & (me >= jnp.where(qq < 64, 1, 2))
    wrap_mask = (kk >= 64) | (me == PLANE - 1)

    def rows_of(ref, g):
        return [ref[i : i + 1, :] for i in (2 * g, 2 * g + 1, 8 + 2 * g, 9 + 2 * g)]

    def own(ref, g):
        return ref[:, :, pl.ds(g * W, W)].reshape(2 * BLK, W)

    def own_map(ref, g, m):
        return ref[:, :, map_cols(g, m)].reshape(2 * BLK, 128)

    def first(ref, g):
        both = ref[g].reshape(2 * BLK, 128 + W)
        return both[:, :128], both[:, 128:]

    def second(ref, g):
        return ref[g].reshape(2 * BLK, 128)

    def out_cols(g):
        return pl.ds(pl.multiple_of((hd * HG + g) * W, W), W)

    def rows_at(h):
        return pl.ds(pl.multiple_of(h * ROWS, ROWS), ROWS)

    def spread(stage, dst, g, i):
        for d in range(1, NH):
            pltpu.make_async_remote_copy(
                src_ref=stage.at[g, :, rows_at(head(d)), :], dst_ref=dst.at[:, :, out_cols(g)],
                send_sem=r_send.at[i, g], recv_sem=r_recv.at[i],
                device_id=(me, head(d)), device_id_type=MESH,
            ).start()
        pltpu.make_async_copy(
            stage.at[g, :, rows_at(hd), :], dst.at[:, :, out_cols(g)], out_sem.at[i]
        ).start()

    def give_back(stage, dst, g, c, send, recv):
        for d in range(NH):
            pltpu.make_async_remote_copy(
                src_ref=stage.at[rows_at(head(d)), :], dst_ref=dst.at[:, out_cols(g)],
                send_sem=send, recv_sem=recv,
                device_id=(c, head(d)), device_id_type=MESH,
            ).start()

    own_q = pq.at[pl.ds(0, 2)]
    lam_tile[...] = jnp.zeros((8, 128), F32)
    for g in range(HG):
        q0, q1, do = own_map(q_v, g, 0), own_map(q_v, g, 1), own(do_v, g)
        k0, k1, v = own_map(k_v, g, 0), own_map(k_v, g, 1), own(v_v, g)
        p1, inner, lam_row = second_map(q1, do, k1, v, rows_of(nd, g), own_mask)
        dq, dk, dv = gradients(p1, inner, q0, q1, do, k0, k1, rows_of(nd, g), lam_s[g], own_mask)
        st_q[g] = rounded(dq)
        acc_k[g] = dk
        acc_v[g] = dv
        lam_tile[g : g + 1, :] = lam_row
        spread(st_q, own_q, g, 0)

    for s in (1, 2):

        @pl.when(behind(s))
        def _():
            wait_for(rnd.at[s - 1], nd_recv.at[s - 1])

    left = lax.broadcasted_iota(jnp.int32, (16, 128), 1) < BLK
    ndr[...] = jnp.where(left, pltpu.roll(rnd[0], BLK, 1), rnd[1])

    for g in range(HG):
        for s in (1, 2):

            @pl.when(behind(s))
            def _():
                wait_for(r_a.at[g, s - 1], a_recv.at[s - 1, g])

        q1, do = first(r_a, g)
        r_p1[g], r_in[g], lam_row = second_map(q1, do, own_map(k_v, g, 1), own(v_v, g), rows_of(ndr, g), rem_mask)
        lam_tile[g : g + 1, :] += lam_row

    @pl.when(z == 0)
    def _():
        pl.semaphore_wait(line_sem.at[0], DEPTH - 1)
        for d in range(1, DEPTH):
            pl.semaphore_signal(line_sem.at[1], inc=1, device_id=(line(d), hd), device_id_type=MESH)

    def sum_over_plane():
        lbuf1[r8] = lam_tile[...]
        for d in range(1, PLANE):
            pltpu.make_async_remote_copy(
                src_ref=lbuf1.at[r8], dst_ref=lbuf1.at[r8],
                send_sem=l_send.at[0], recv_sem=l_recv.at[0],
                device_id=(z * PLANE + lax.rem(r8 + d, PLANE), hd), device_id_type=MESH,
            ).start()
        pass

    def sum_over_line():
        @pl.when(z > 0)
        def _():
            pl.semaphore_wait(line_sem.at[1], 1)

        wait_for(lbuf1.at[pl.ds(0, PLANE - 1)], l_recv.at[0])
        total = lbuf1[0]
        for i in range(1, PLANE):
            total = total + lbuf1[i]
        lbuf2[z] = total
        for d in range(1, DEPTH):
            pltpu.make_async_remote_copy(
                src_ref=lbuf2.at[z], dst_ref=lbuf2.at[z],
                send_sem=l_send.at[1], recv_sem=l_recv.at[1],
                device_id=(line(d), hd), device_id_type=MESH,
            ).start()

    @pl.when(z > 0)
    def _():
        sum_over_plane()

    for g in range(HG):
        for s in (1, 2):

            @pl.when(behind(s))
            def _():
                wait_for(r_b.at[g, s - 1], b_recv.at[s - 1, g])

        q1, do = first(r_a, g)
        dq, dk, dv = gradients(
            r_p1[g], r_in[g], second(r_b, g), q1, do, own_map(k_v, g, 0), own_map(k_v, g, 1),
            rows_of(ndr, g), lam_s[g], rem_mask,
        )
        st_p[g] = rounded(dq)
        st_k[g] = rounded(acc_k[g] + dk)
        st_v[g] = rounded(acc_v[g] + dv)
        for s in (1, 2):

            @pl.when(behind(s))
            def _():
                give_back(st_p.at[g, s - 1], pq.at[s + 1], g, ctx(-s), p_send.at[s - 1, g], p_recv.at[s - 1])

        spread(st_k, lk, g, 1)
        spread(st_v, lv, g, 2)
        if g == 1:

            @pl.when(z > 0)
            def _():
                sum_over_line()

    @pl.when(host)
    def _():
        wait_for(h_nd, hn_recv)
        for g in range(HG):
            wait_for(h_a.at[g], ha_recv.at[g])
            for s in (1, 2):

                @pl.when(hosts(s))
                def _():
                    wait_for(w_a.at[g, s - 1], wa_recv.at[s - 1, g])

            q1, do = first(h_a, g)
            k1, v = first(w_a, g)
            w_p1[g], w_in[g], lam_row = second_map(q1, do, k1, v, rows_of(h_nd, g), wrap_mask)
            lam_tile[g : g + 1, :] += lam_row

    @pl.when(z == 0)
    def _():
        sum_over_plane()

    @pl.when(host)
    def _():
        pl.semaphore_wait(line_sem.at[2], NH)
        for g in range(HG):
            wait_for(h_b.at[g], hb_recv.at[g])
            for s in (1, 2):

                @pl.when(hosts(s))
                def _():
                    wait_for(w_b.at[g, s - 1], wb_recv.at[s - 1, g])

            q1, do = first(h_a, g)
            k1, v = first(w_a, g)
            dq, dk, dv = gradients(
                w_p1[g], w_in[g], second(h_b, g), q1, do, second(w_b, g), k1, rows_of(h_nd, g), lam_s[g], wrap_mask
            )
            st_wq[g] = rounded(dq)
            st_wk[g] = rounded(dk)
            st_wv[g] = rounded(dv)
            for d in heads:
                pltpu.make_async_remote_copy(
                    src_ref=st_wq.at[g, :, rows_at(head(d)), :], dst_ref=wq.at[:, :, out_cols(g)],
                    send_sem=wq_send.at[g], recv_sem=wq_recv,
                    device_id=(guest, head(d)), device_id_type=MESH,
                ).start()
            for s in (1, 2):

                @pl.when(hosts(s))
                def _():
                    to = me + s - PLANE
                    give_back(st_wk.at[g, s - 1], wk.at[s - 1], g, to, pw_send.at[s - 1, g, 0], pw_recv.at[s - 1, 0])
                    give_back(st_wv.at[g, s - 1], wv.at[s - 1], g, to, pw_send.at[s - 1, g, 1], pw_recv.at[s - 1, 1])

    @pl.when(z == 0)
    def _():
        sum_over_line()

    part = pl.ds(0, (NH - 1) * HG * W)
    for i, (dst, stage) in enumerate(((own_q, st_q), (lk, st_k), (lv, st_v))):
        wait_for(dst.at[:, :, part], r_recv.at[i])
        for g in range(HG):
            wait_for(stage.at[g, :, pl.ds(0, ROWS)], out_sem.at[i])
    for s in (1, 2):

        @pl.when(ahead(s))
        def _():
            wait_for(pq.at[s + 1], p_recv.at[s - 1])

        @pl.when(~behind(s))
        def _():
            for i, (dst, term) in enumerate(((lk, wk), (lv, wv))):
                wait_for(term.at[s - 1], pw_recv.at[s - 1, i])

    @pl.when(me == 0)
    def _():
        for dst, term in ((lk, wk), (lv, wv)):
            dst[0] = (dst[0].astype(F32) + term[0].astype(F32) + term[1].astype(F32)).astype(BF16)

    @pl.when(me == 1)
    def _():
        for dst, term in ((lk, wk), (lv, wv)):
            dst[0] = (dst[0].astype(F32) + term[1].astype(F32)).astype(BF16)

    @pl.when(last_two)
    def _():
        wait_for(wq, wq_recv)
        pq[0] = (pq[0].astype(F32) + wq[0].astype(F32)).astype(BF16)
        pq[3] = wq[1]


    sent = (q_v.at[0, :, pl.ds(0, HG * 128)], q_v.at[0])
    for s in (1, 2):

        @pl.when(ahead(s))
        def _():
            wait_for(sent[0], qs_send.at[s - 1, 0])
            wait_for(sent[1], qs_send.at[s - 1, 1])
            wait_for(sent[0], qs_send.at[s - 1, 2])
            wait_for(nd, nd_send.at[s - 1])
            pass

        @pl.when(~behind(s))
        def _():
            wait_for(sent[0], ws_send.at[s - 1, 0])
            wait_for(sent[1], ws_send.at[s - 1, 1])
            wait_for(sent[0], ws_send.at[s - 1, 2])
            pass

        for g in range(HG):

            @pl.when(behind(s))
            def _():
                wait_for(st_p.at[g, s - 1], p_send.at[s - 1, g])

            @pl.when(hosts(s))
            def _():
                wait_for(st_wk.at[g, s - 1], pw_send.at[s - 1, g, 0])
                wait_for(st_wv.at[g, s - 1], pw_send.at[s - 1, g, 1])

    @pl.when(host)
    def _():
        for g in range(HG):
            wait_for(st_wq.at[g], wq_send.at[g])
        pass

    @pl.when(last_two)
    def _():
        both = q_v.at[:, :, pl.ds(0, HG * 128)]
        wait_for(both, hs_send.at[0])
        wait_for(q_v, hs_send.at[1])
        wait_for(nd, hs_send.at[2])
        wait_for(both, hs_send.at[3])
        pass

    for i, stage in enumerate((st_q, st_k, st_v)):
        for g in range(HG):
            wait_for(stage.at[g, :, pl.ds(0, (NH - 1) * ROWS)], r_send.at[i, g])
    wait_for(lbuf1.at[pl.ds(0, PLANE - 1)], l_send.at[0])
    wait_for(lbuf2.at[pl.ds(0, DEPTH - 1)], l_recv.at[1])
    wait_for(lbuf2.at[pl.ds(0, DEPTH - 1)], l_send.at[1])


def finish_kernel(pq, lk, lv, lbuf2, oq, ok, ov, lam_out, sum_q, sems):
    copies = [
        pltpu.make_async_copy(lk, ok, sems.at[0]),
        pltpu.make_async_copy(lv, ov, sems.at[1]),
        pltpu.make_async_copy(pq.at[0], oq.at[0], sems.at[2]),
        pltpu.make_async_copy(sum_q, oq.at[1], sems.at[3]),
    ]
    for c in copies[:3]:
        c.start()
    sum_q[...] = (pq[1].astype(F32) + pq[2].astype(F32) + pq[3].astype(F32)).astype(BF16)
    copies[3].start()
    total = lbuf2[0]
    for i in range(1, DEPTH):
        total = total + lbuf2[i]
    for g in range(HG):
        lam_out[g] = -jnp.sum(total[g : g + 1, :])
    for c in copies:
        c.wait()


def local(query_rows, key_rows, value_rows, out_grad, log_norms, row_deltas, lambdas):
    n = lax.axis_size("ctx")
    hbm = pl.BlockSpec(memory_space=pl.ANY)
    vmem = pl.BlockSpec(memory_space=pltpu.VMEM)
    smem = pl.BlockSpec(memory_space=pltpu.SMEM)
    half = (2, BLK, HG * W)
    tile = (HG, 2, BLK, W)
    dma, regular = pltpu.SemaphoreType.DMA, pltpu.SemaphoreType.REGULAR
    args = (
        query_rows, key_rows, value_rows, out_grad,
        jnp.swapaxes(log_norms, 1, 2), jnp.swapaxes(row_deltas, 1, 2), lambdas,
    )
    pq, lk, lv, sums = pl.pallas_call(
        functools.partial(main_kernel, n),
        out_shape=(
            pltpu.VMEM((4, ROWS, COLS), BF16),
            pltpu.VMEM((2, ROWS, COLS), BF16), pltpu.VMEM((2, ROWS, COLS), BF16),
            pltpu.VMEM((DEPTH, 8, 128), F32),
        ),
        in_specs=[hbm] * 7,
        out_specs=(vmem,) * 4,
        scratch_shapes=[
            pltpu.SMEM((HG,), F32),
            pltpu.VMEM(half, BF16), pltpu.VMEM(half, BF16), pltpu.VMEM(half, BF16), pltpu.VMEM(half, BF16),
            pltpu.VMEM((2, HG, 2, BLK), F32), pltpu.VMEM((2, HG, 2, BLK), F32),
            pltpu.VMEM((16, 128), F32), pltpu.VMEM((16, 128), F32), pltpu.VMEM((2, 16, 128), F32),
            *[pltpu.VMEM((HG, 2, BLK, c), BF16) for c in (128 + W, 128) * 3],
            pltpu.VMEM((16, 128), F32),
            *[pltpu.VMEM((HG, 2 * BLK, 2 * BLK), F32) for _ in range(4)],
            *[pltpu.VMEM((HG, 2 * BLK, W), F32) for _ in range(2)],
            *[pltpu.VMEM(tile, BF16) for _ in range(7)],
            *[pltpu.VMEM((2, ROWS, COLS), BF16) for _ in range(3)],
            pltpu.VMEM((8, 128), F32), pltpu.VMEM((PLANE, 8, 128), F32),
            dma((7,)), dma((3,)), dma((2, 3)), dma((2, HG)), dma((2, HG)), dma((2,)), dma((2,)),
            dma((2, 3)), dma((2, HG)), dma((2, HG)),
            dma((4,)), dma((HG,)), dma((HG,)), dma, dma((HG,)), dma,
            dma((3, HG)), dma((3,)), dma((2, HG)), dma((2,)), dma((2, HG, 2)), dma((2, 2)), dma((2,)), dma((2,)),
            regular((3,)),
        ],
        compiler_params=pltpu.CompilerParams(
            collective_id=0, has_side_effects=True, vmem_limit_bytes=24 * 1024 * 1024
        ),
        cost_estimate=pl.CostEstimate(flops=3 * 10**8, bytes_accessed=2 * 10**6, transcendentals=2 * 10**5),
        name="attention_backward",
    )(*[pltpu.with_memory_space_constraint(x, pltpu.HBM) for x in args])
    out = jax.ShapeDtypeStruct((2, ROWS, COLS), BF16)
    return pl.pallas_call(
        finish_kernel,
        out_shape=(out, out, out, jax.ShapeDtypeStruct((HG,), F32)),
        in_specs=[vmem] * 4,
        out_specs=(hbm, hbm, hbm, smem),
        scratch_shapes=[pltpu.VMEM((ROWS, COLS), BF16), dma((4,))],
        compiler_params=pltpu.CompilerParams(vmem_limit_bytes=16 * 1024 * 1024),
        name="write_outputs",
    )(*[pltpu.with_memory_space_constraint(x, pltpu.VMEM) for x in (pq, lk, lv, sums)])


def solution(mesh):
    in_specs = (
        P(None, "ctx", "head"),
        P(None, "ctx", "head"),
        P(None, "ctx", "head"),
        P(None, "ctx", "head"),
        P(None, None, "head", "ctx"),
        P(None, None, "head", "ctx"),
        P("head"),
    )
    out_specs = (
        P(None, ("ctx", "head"), None),
        P(None, ("ctx", "head"), None),
        P(None, ("ctx", "head"), None),
        P("head"),
    )
    return jax.shard_map(local, mesh=mesh, in_specs=in_specs, out_specs=out_specs, check_vma=False)
```

```python
import functools
import math

import jax
import jax.numpy as jnp
from jax import lax
from jax.experimental import pallas as pl
from jax.experimental.pallas import tpu as pltpu
from jax.sharding import PartitionSpec as P

MESH = pl.DeviceIdType.MESH
F32, BF16 = jnp.float32, jnp.bfloat16
HG = 3
BLK = 64
NH = 4
ROWS = BLK // NH
W = 256
COLS = NH * HG * W
PLANE = 8
DEPTH = 16
EARLY = 4
SCALE = 1.0 / math.sqrt(128.0)


def nt(a, b):
    return lax.dot_general(a, b, (((1,), (1,)), ((), ())), preferred_element_type=F32)


def nn(a, b):
    return lax.dot_general(a, b, (((1,), (0,)), ((), ())), preferred_element_type=F32)


def tn(a, b):
    return lax.dot_general(a, b, (((0,), (0,)), ((), ())), preferred_element_type=F32)


def second_map(q1, do, k1, v, rows, mask):
    inner = nt(v, do)
    p1 = jnp.where(mask, jnp.exp(nt(k1, q1) * SCALE - rows[1]), 0.0)
    return p1, inner, jnp.sum(p1 * inner, axis=0, keepdims=True)


def gradients(p1, inner, q0, q1, do, k0, k1, rows, lam, mask):
    n0, _, d0, d1 = rows
    p0 = jnp.where(mask, jnp.exp(nt(k0, q0) * SCALE - n0), 0.0)
    mixed = (p0 - lam * p1).astype(BF16)
    g0 = (SCALE * p0 * (inner - d0)).astype(BF16)
    g1 = ((-lam * SCALE) * p1 * (inner - d1)).astype(BF16)
    dv = nn(mixed, do)
    dk = jnp.concatenate([nn(g0, q0), nn(g1, q1)], axis=1)
    dq = jnp.concatenate([tn(g0, k0), tn(g1, k1)], axis=1)
    return dq, dk, dv


def wait_for(ref, sem):
    pltpu.make_async_copy(ref, ref, sem).wait()


def rounded(x):
    return x.astype(BF16).reshape(2, BLK, W)


def main_kernel(
    n,
    q_hbm, k_hbm, v_hbm, do_hbm, norm_hbm, delta_hbm, lam_hbm,
    landed, back, lbuf2,
    lam_s, q_v, k_v, v_v, do_v, nv, dv_, nd, ndr, rnd, r_a, r_b, w_kv, h_qd, h_nd, r_p1, r_in,
    acc, stage, st_p, st_wkv, st_wq, wkv, wq, lam_tile, lbuf1,
    in_sem, own_sem, qs_send, a_recv, b_recv, f_send, nd_send, nd_recv, ws_send, w_recv,
    hs_send, h_recv, hn_recv, wq_send, wq_recv,
    r_send, r_recv, p_send, p_recv, pw_send, pw_recv, l_send, l_recv, line_sem,
):
    me = lax.axis_index("ctx")
    hd = lax.axis_index("head")
    z, r8 = me // PLANE, me % PLANE

    def ctx(d):
        return lax.rem(me + (d + n), n)

    def head(d):
        return lax.rem(hd + d, NH)

    def line(d):
        return lax.rem(z + d, DEPTH) * PLANE + r8

    def ahead(s):
        return me + s < n

    def behind(s):
        return me >= s

    last_two = me >= n - 2
    host = (me >= PLANE - 2) & (me < PLANE)
    guest = me + (n - PLANE)

    def hosts(s):
        return host & (me + s >= PLANE)

    loads = [
        pltpu.make_async_copy(a, b, in_sem.at[i])
        for i, (a, b) in enumerate(
            [(q_hbm, q_v), (do_hbm, do_v), (norm_hbm, nv), (delta_hbm, dv_), (k_hbm, k_v), (v_hbm, v_v), (lam_hbm, lam_s)]
        )
    ]
    for c in loads:
        c.start()

    barrier = pltpu.get_barrier_semaphore()

    def tell(c, h):
        pl.semaphore_signal(barrier, inc=1, device_id=(c, h), device_id_type=MESH)

    heads = range(NH)
    for s in (1, 2):

        @pl.when(behind(s))
        def _():
            for d in heads:
                tell(ctx(-s), head(d))

        @pl.when(ahead(s))
        def _():
            for d in heads:
                tell(ctx(s), head(d))

        @pl.when(~behind(s))
        def _():
            for d in heads:
                tell(me - s + PLANE, head(d))

    for d in range(1, PLANE):
        tell(z * PLANE + lax.rem(r8 + d, PLANE), hd)
    for d in range(1, NH):
        tell(me, head(d))

    @pl.when(z < EARLY)
    def _():
        for d in range(1, DEPTH):
            tell(line(d), hd)

    @pl.when(host)
    def _():
        for d in range(1, NH):
            tell(guest, head(d))

    def when(condition, count):
        return jnp.where(condition, count, 0)

    pl.semaphore_wait(
        barrier,
        sum(when(ahead(s), NH) + when(behind(s), NH) + when(hosts(s), NH) for s in (1, 2))
        + EARLY - when(z < EARLY, 1) + when(last_two, NH - 1) + (NH - 1) + (PLANE - 1),
    )

    @pl.when(z > 0)
    def _():
        pl.semaphore_signal(line_sem.at[0], inc=1, device_id=(r8, hd), device_id_type=MESH)

    @pl.when(last_two)
    def _():
        for d in heads:
            pl.semaphore_signal(line_sem.at[2], inc=1, device_id=(r8, head(d)), device_id_type=MESH)

    def map_cols(g, m):
        return pl.ds(g * W + m * 128, 128)

    def send_first(g, s):
        for i, (ref, cols, lanes) in enumerate(
            ((q_v, map_cols(g, 1), pl.ds(0, 128)), (do_v, pl.ds(g * W, W), pl.ds(128, W)))
        ):
            pltpu.make_async_remote_copy(
                src_ref=ref.at[1, :, cols], dst_ref=r_a.at[g, s - 1, :, lanes],
                send_sem=qs_send.at[s - 1, i], recv_sem=a_recv.at[s - 1, g],
                device_id=(ctx(s), hd), device_id_type=MESH,
            ).start()

    def send_second(g, s):
        pltpu.make_async_remote_copy(
            src_ref=q_v.at[1, :, map_cols(g, 0)], dst_ref=r_b.at[g, s - 1],
            send_sem=qs_send.at[s - 1, 2], recv_sem=b_recv.at[s - 1, g],
            device_id=(ctx(s), hd), device_id_type=MESH,
        ).start()

    def send_nd(dst, c, send, recv):
        pltpu.make_async_remote_copy(
            src_ref=nd, dst_ref=dst, send_sem=send, recv_sem=recv, device_id=(c, hd), device_id_type=MESH
        ).start()

    for c in loads:
        c.wait()
    for half in range(2):
        lanes = pl.ds(half * BLK, BLK)
        for i in range(HG):
            nd[2 * i : 2 * i + 2, lanes] = nv[half, i]
            nd[8 + 2 * i : 10 + 2 * i, lanes] = dv_[half, i]

    @pl.when(last_two)
    def _():
        send_nd(h_nd, r8, hs_send.at[2], hn_recv)
        for g in range(HG):
            for i, ref in enumerate((q_v, do_v)):
                pltpu.make_async_remote_copy(
                    src_ref=ref.at[:, :, pl.ds(g * W, W)], dst_ref=h_qd.at[g, :, :, pl.ds(i * W, W)],
                    send_sem=hs_send.at[i], recv_sem=h_recv.at[g],
                    device_id=(r8, hd), device_id_type=MESH,
                ).start()

    for s in (1, 2):

        @pl.when(ahead(s))
        def _():
            send_nd(rnd.at[s - 1], ctx(s), nd_send.at[s - 1], nd_recv.at[s - 1])

    odd = r8 % 2 == 1
    for g in range(HG):
        for s in (2, 1):

            @pl.when(ahead(s) & ~odd if g == 0 and s == 1 else ahead(s))
            def _():
                send_first(g, s)

    for s in (1, 2):

        @pl.when(~behind(s))
        def _():
            for g in range(HG):
                for i, ref in enumerate((k_v, v_v)):
                    pltpu.make_async_remote_copy(
                        src_ref=ref.at[0, :, pl.ds(g * W, W)], dst_ref=w_kv.at[g, s - 1, :, pl.ds(i * W, W)],
                        send_sem=ws_send.at[s - 1, i], recv_sem=w_recv.at[s - 1, g],
                        device_id=(me - s + PLANE, hd), device_id_type=MESH,
                    ).start()


    for s in (1, 2):

        @pl.when(~behind(s))
        def _():
            r_a[:, s - 1] = jnp.zeros((HG, BLK, 128 + W), BF16)
            r_b[:, s - 1] = jnp.zeros((HG, BLK, 128), BF16)
            rnd[s - 1] = jnp.zeros((16, 128), F32)

    @pl.when(me == PLANE - 2)
    def _():
        w_kv[:, 0] = jnp.zeros((HG, BLK, 2 * W), BF16)

    @pl.when(me == n - 1)
    def _():
        back[0] = jnp.zeros((ROWS, COLS), BF16)

    kk = lax.broadcasted_iota(jnp.int32, (128, 128), 0)
    qq = lax.broadcasted_iota(jnp.int32, (128, 128), 1)
    own_mask = ((kk < 64) & (qq >= 64)) | (((kk < 64) == (qq < 64)) & (kk <= qq))
    rem_mask = (kk < 64) | (qq < 64) | (me >= 2)
    rem_mask = rem_mask & (me >= jnp.where(qq < 64, 1, 2))
    wrap_mask = (kk >= 64) | (me == PLANE - 1)

    def rows_of(ref, g):
        return [ref[i : i + 1, :] for i in (2 * g, 2 * g + 1, 8 + 2 * g, 9 + 2 * g)]

    def own(ref, g):
        return ref[:, :, pl.ds(g * W, W)].reshape(2 * BLK, W)

    def own_map(ref, g, m):
        return ref[:, :, map_cols(g, m)].reshape(2 * BLK, 128)

    def first(ref, g):
        both = ref[g].reshape(2 * BLK, 128 + W)
        return both[:, :128], both[:, 128:]

    def second(ref, g):
        return ref[g].reshape(2 * BLK, 128)

    def pair(ref, g):
        both = ref[g].reshape(2 * BLK, 2 * W)
        return both[:, :128], both[:, 128:W], both[:, W:]

    def out_cols(g):
        return pl.ds(pl.multiple_of((hd * HG + g) * W, W), W)

    def rows_at(h):
        return pl.ds(pl.multiple_of(h * ROWS, ROWS), ROWS)

    def spread(g):
        for d in range(1, NH):
            pltpu.make_async_remote_copy(
                src_ref=stage.at[g, :, rows_at(head(d)), :], dst_ref=landed.at[:, :, out_cols(g)],
                send_sem=r_send.at[g], recv_sem=r_recv,
                device_id=(me, head(d)), device_id_type=MESH,
            ).start()
        pltpu.make_async_copy(
            stage.at[g, :, rows_at(hd), :], landed.at[:, :, out_cols(g)], own_sem
        ).start()
        pass

    lam_tile[...] = jnp.zeros((8, 128), F32)
    for g in range(HG):
        q0, q1, do = own_map(q_v, g, 0), own_map(q_v, g, 1), own(do_v, g)
        k0, k1, v = own_map(k_v, g, 0), own_map(k_v, g, 1), own(v_v, g)
        p1, inner, lam_row = second_map(q1, do, k1, v, rows_of(nd, g), own_mask)
        dq, dk, dv = gradients(p1, inner, q0, q1, do, k0, k1, rows_of(nd, g), lam_s[g], own_mask)
        stage[g, 0:2] = rounded(dq)
        acc[g, 0] = dk
        acc[g, 1] = dv
        lam_tile[g : g + 1, :] = lam_row

    sent = [q_v.at[0, :, pl.ds(0, c)] for c in (HG * 128, HG * W, (HG - 1) * 128, (HG - 1) * W)]
    relays = odd & behind(2)

    @pl.when(relays)
    def _():
        wait_for(r_a.at[0, 1], a_recv.at[1, 0])
        pltpu.make_async_remote_copy(
            src_ref=r_a.at[0, 1], dst_ref=r_a.at[0, 0], send_sem=f_send, recv_sem=a_recv.at[0, 0],
            device_id=(ctx(-1), hd), device_id_type=MESH,
        ).start()

    for s in (1, 2):

        @pl.when(ahead(s) & ~odd if s == 1 else ahead(s))
        def _():
            wait_for(sent[0], qs_send.at[s - 1, 0])
            wait_for(sent[1], qs_send.at[s - 1, 1])

        if s == 1:

            @pl.when(ahead(s) & odd)
            def _():
                wait_for(sent[2], qs_send.at[0, 0])
                wait_for(sent[3], qs_send.at[0, 1])

        @pl.when(ahead(s))
        def _():
            for g in range(HG):
                send_second(g, s)


    for s in (1, 2):

        @pl.when(behind(s))
        def _():
            wait_for(rnd.at[s - 1], nd_recv.at[s - 1])

    left = lax.broadcasted_iota(jnp.int32, (16, 128), 1) < BLK
    ndr[...] = jnp.where(left, pltpu.roll(rnd[0], BLK, 1), rnd[1])

    for g in range(HG):
        for s in (1, 2):

            @pl.when(behind(s) & ~relays if g == 0 and s == 2 else behind(s))
            def _():
                wait_for(r_a.at[g, s - 1], a_recv.at[s - 1, g])

        q1, do = first(r_a, g)
        r_p1[g], r_in[g], lam_row = second_map(q1, do, own_map(k_v, g, 1), own(v_v, g), rows_of(ndr, g), rem_mask)
        lam_tile[g : g + 1, :] += lam_row

    def sum_over_plane():
        lbuf1[r8] = lam_tile[...]
        for d in range(1, PLANE):
            pltpu.make_async_remote_copy(
                src_ref=lbuf1.at[r8], dst_ref=lbuf1.at[r8],
                send_sem=l_send.at[0], recv_sem=l_recv.at[0],
                device_id=(z * PLANE + lax.rem(r8 + d, PLANE), hd), device_id_type=MESH,
            ).start()
        pass

    def sum_over_line():
        wait_for(lbuf1.at[pl.ds(0, PLANE - 1)], l_recv.at[0])
        total = lbuf1[0]
        for i in range(1, PLANE):
            total = total + lbuf1[i]
        lbuf2[z] = total

        def send_sum(to):
            @pl.when(z != to)
            def _():
                pltpu.make_async_remote_copy(
                    src_ref=lbuf2.at[z], dst_ref=lbuf2.at[z],
                    send_sem=l_send.at[1], recv_sem=l_recv.at[1],
                    device_id=(to * PLANE + r8, hd), device_id_type=MESH,
                ).start()

        for to in range(EARLY):
            send_sum(to)

        @pl.when(z > 0)
        def _():
            pl.semaphore_wait(line_sem.at[1], 1)

        for to in range(EARLY, DEPTH):
            send_sum(to)

    @pl.when(z > 0)
    def _():
        sum_over_plane()

    for g in range(HG):
        for s in (1, 2):

            @pl.when(behind(s))
            def _():
                wait_for(r_b.at[g, s - 1], b_recv.at[s - 1, g])

        q1, do = first(r_a, g)
        dq, dk, dv = gradients(
            r_p1[g], r_in[g], second(r_b, g), q1, do, own_map(k_v, g, 0), own_map(k_v, g, 1),
            rows_of(ndr, g), lam_s[g], rem_mask,
        )
        for s in (1, 2):
            st_p[s - 1, :, pl.ds(g * W, W)] = rounded(dq)[s - 1]
        stage[g, 2:4] = rounded(acc[g, 0] + dk)
        stage[g, 4:6] = rounded(acc[g, 1] + dv)
        spread(g)
        if g == 1:

            @pl.when(z > 0)
            def _():
                sum_over_line()

    all_cols = pl.ds(pl.multiple_of(hd * HG * W, W), HG * W)
    for s in (1, 2):

        @pl.when(behind(s))
        def _():
            for d in heads:
                pltpu.make_async_remote_copy(
                    src_ref=st_p.at[s - 1, rows_at(head(d)), :], dst_ref=back.at[s - 1, :, all_cols],
                    send_sem=p_send.at[s - 1], recv_sem=p_recv.at[s - 1],
                    device_id=(ctx(-s), head(d)), device_id_type=MESH,
                ).start()


    @pl.when(host)
    def _():
        pl.semaphore_wait(line_sem.at[2], NH)
        wait_for(h_nd, hn_recv)
        for g in range(HG):
            for s in (1, 2):

                @pl.when(hosts(s))
                def _():
                    wait_for(w_kv.at[g, s - 1], w_recv.at[s - 1, g])

            wait_for(h_qd.at[g], h_recv.at[g])
            q0, q1, do = pair(h_qd, g)
            k0, k1, v = pair(w_kv, g)
            p1, inner, lam_row = second_map(q1, do, k1, v, rows_of(h_nd, g), wrap_mask)
            lam_tile[g : g + 1, :] += lam_row
            dq, dk, dv = gradients(p1, inner, q0, q1, do, k0, k1, rows_of(h_nd, g), lam_s[g], wrap_mask)
            st_wq[g] = rounded(dq)
            for s in (1, 2):
                st_wkv[g, s - 1, 0] = rounded(dk)[s - 1]
                st_wkv[g, s - 1, 1] = rounded(dv)[s - 1]
            for s in (1, 2):

                @pl.when(hosts(s))
                def _():
                    for d in heads:
                        pltpu.make_async_remote_copy(
                            src_ref=st_wkv.at[g, s - 1, :, rows_at(head(d)), :],
                            dst_ref=wkv.at[s - 1, :, :, out_cols(g)],
                            send_sem=pw_send.at[s - 1, g], recv_sem=pw_recv.at[s - 1],
                            device_id=(me + s - PLANE, head(d)), device_id_type=MESH,
                        ).start()

            for d in heads:
                pltpu.make_async_remote_copy(
                    src_ref=st_wq.at[g, :, rows_at(head(d)), :], dst_ref=wq.at[:, :, out_cols(g)],
                    send_sem=wq_send.at[g], recv_sem=wq_recv,
                    device_id=(guest, head(d)), device_id_type=MESH,
                ).start()

    @pl.when(z == 0)
    def _():
        sum_over_plane()

    @pl.when(z == 0)
    def _():
        pl.semaphore_wait(line_sem.at[0], DEPTH - 1)
        for d in range(1, DEPTH):
            pl.semaphore_signal(line_sem.at[1], inc=1, device_id=(line(d), hd), device_id_type=MESH)

    @pl.when(z == 0)
    def _():
        sum_over_line()

    wait_for(landed.at[:, :, pl.ds(0, (NH - 1) * HG * W)], r_recv)
    for g in range(HG):
        wait_for(stage.at[g, :, pl.ds(0, ROWS)], own_sem)
    for s in (1, 2):

        @pl.when(ahead(s))
        def _():
            wait_for(back.at[s - 1], p_recv.at[s - 1])

        @pl.when(~behind(s))
        def _():
            wait_for(wkv.at[s - 1], pw_recv.at[s - 1])

    @pl.when(me < 2)
    def _():
        for i in range(2):
            first_term = jnp.where(me == 0, wkv[0, i].astype(F32), 0.0)
            total = landed[2 + 2 * i].astype(F32) + first_term + wkv[1, i].astype(F32)
            landed[2 + 2 * i] = total.astype(BF16)

    @pl.when(last_two)
    def _():
        wait_for(wq, wq_recv)
        landed[0] = (landed[0].astype(F32) + wq[0].astype(F32)).astype(BF16)
        back[1] = wq[1]


    for s in (1, 2):

        @pl.when(ahead(s))
        def _():
            wait_for(sent[0], qs_send.at[s - 1, 2])
            wait_for(nd, nd_send.at[s - 1])
            pass

        @pl.when(~behind(s))
        def _():
            wait_for(sent[1], ws_send.at[s - 1, 0])
            wait_for(sent[1], ws_send.at[s - 1, 1])
            pass

        @pl.when(behind(s))
        def _():
            wait_for(st_p.at[s - 1], p_send.at[s - 1])

        @pl.when(hosts(s))
        def _():
            for g in range(HG):
                wait_for(st_wkv.at[g, s - 1], pw_send.at[s - 1, g])


    @pl.when(relays)
    def _():
        wait_for(r_a.at[0, 1], f_send)

    @pl.when(host)
    def _():
        for g in range(HG):
            wait_for(st_wq.at[g], wq_send.at[g])
        pass

    @pl.when(last_two)
    def _():
        wait_for(q_v, hs_send.at[0])
        wait_for(q_v, hs_send.at[1])
        wait_for(nd, hs_send.at[2])
        pass

    for g in range(HG):
        wait_for(stage.at[g, :, pl.ds(0, (NH - 1) * ROWS)], r_send.at[g])
    wait_for(lbuf1.at[pl.ds(0, PLANE - 1)], l_send.at[0])
    wait_for(lbuf2.at[pl.ds(0, DEPTH - 1)], l_recv.at[1])
    wait_for(lbuf2.at[pl.ds(0, DEPTH - 1)], l_send.at[1])


def finish_kernel(landed, back, lbuf2, oq, ok, ov, lam_out, sum_q, sems):
    copies = [
        pltpu.make_async_copy(landed.at[pl.ds(2, 2)], ok, sems.at[0]),
        pltpu.make_async_copy(landed.at[pl.ds(4, 2)], ov, sems.at[1]),
        pltpu.make_async_copy(landed.at[0], oq.at[0], sems.at[2]),
        pltpu.make_async_copy(sum_q, oq.at[1], sems.at[3]),
    ]
    for c in copies[:3]:
        c.start()
    sum_q[...] = (landed[1].astype(F32) + back[0].astype(F32) + back[1].astype(F32)).astype(BF16)
    copies[3].start()
    total = lbuf2[0]
    for i in range(1, DEPTH):
        total = total + lbuf2[i]
    for g in range(HG):
        lam_out[g] = -jnp.sum(total[g : g + 1, :])
    for c in copies:
        c.wait()


def local(query_rows, key_rows, value_rows, out_grad, log_norms, row_deltas, lambdas):
    n = lax.axis_size("ctx")
    hbm = pl.BlockSpec(memory_space=pl.ANY)
    vmem = pl.BlockSpec(memory_space=pltpu.VMEM)
    smem = pl.BlockSpec(memory_space=pltpu.SMEM)
    half = (2, BLK, HG * W)
    dma, regular = pltpu.SemaphoreType.DMA, pltpu.SemaphoreType.REGULAR
    args = (
        query_rows, key_rows, value_rows, out_grad,
        jnp.swapaxes(log_norms, 1, 2), jnp.swapaxes(row_deltas, 1, 2), lambdas,
    )
    landed, back, sums = pl.pallas_call(
        functools.partial(main_kernel, n),
        out_shape=(
            pltpu.VMEM((6, ROWS, COLS), BF16), pltpu.VMEM((2, ROWS, COLS), BF16),
            pltpu.VMEM((DEPTH, 8, 128), F32),
        ),
        in_specs=[hbm] * 7,
        out_specs=(vmem,) * 3,
        scratch_shapes=[
            pltpu.SMEM((HG,), F32),
            pltpu.VMEM(half, BF16), pltpu.VMEM(half, BF16), pltpu.VMEM(half, BF16), pltpu.VMEM(half, BF16),
            pltpu.VMEM((2, HG, 2, BLK), F32), pltpu.VMEM((2, HG, 2, BLK), F32),
            pltpu.VMEM((16, 128), F32), pltpu.VMEM((16, 128), F32), pltpu.VMEM((2, 16, 128), F32),
            *[pltpu.VMEM((HG, 2, BLK, c), BF16) for c in (128 + W, 128, 2 * W, 2 * W)],
            pltpu.VMEM((16, 128), F32),
            *[pltpu.VMEM((HG, 2 * BLK, 2 * BLK), F32) for _ in range(2)],
            pltpu.VMEM((HG, 2, 2 * BLK, W), F32), pltpu.VMEM((HG, 6, BLK, W), BF16),
            pltpu.VMEM((2, BLK, HG * W), BF16),
            pltpu.VMEM((HG, 2, 2, BLK, W), BF16), pltpu.VMEM((HG, 2, BLK, W), BF16),
            pltpu.VMEM((2, 2, ROWS, COLS), BF16), pltpu.VMEM((2, ROWS, COLS), BF16),
            pltpu.VMEM((8, 128), F32), pltpu.VMEM((PLANE, 8, 128), F32),
            dma((7,)), dma, dma((2, 3)), dma((2, HG)), dma((2, HG)), dma, dma((2,)), dma((2,)),
            dma((2, 2)), dma((2, HG)), dma((3,)), dma((HG,)), dma, dma((HG,)), dma,
            dma((HG,)), dma, dma((2,)), dma((2,)), dma((2, HG)), dma((2,)), dma((2,)), dma((2,)),
            regular((3,)),
        ],
        compiler_params=pltpu.CompilerParams(
            collective_id=0, has_side_effects=True, vmem_limit_bytes=24 * 1024 * 1024
        ),
        cost_estimate=pl.CostEstimate(flops=3 * 10**8, bytes_accessed=2 * 10**6, transcendentals=2 * 10**5),
        name="attention_backward",
    )(*[pltpu.with_memory_space_constraint(x, pltpu.HBM) for x in args])
    out = jax.ShapeDtypeStruct((2, ROWS, COLS), BF16)
    return pl.pallas_call(
        finish_kernel,
        out_shape=(out, out, out, jax.ShapeDtypeStruct((HG,), F32)),
        in_specs=[vmem] * 3,
        out_specs=(hbm, hbm, hbm, smem),
        scratch_shapes=[pltpu.VMEM((ROWS, COLS), BF16), dma((4,))],
        compiler_params=pltpu.CompilerParams(vmem_limit_bytes=16 * 1024 * 1024),
        name="write_outputs",
    )(*[pltpu.with_memory_space_constraint(x, pltpu.VMEM) for x in (landed, back, sums)])


def solution(mesh):
    in_specs = (
        P(None, "ctx", "head"),
        P(None, "ctx", "head"),
        P(None, "ctx", "head"),
        P(None, "ctx", "head"),
        P(None, None, "head", "ctx"),
        P(None, None, "head", "ctx"),
        P("head"),
    )
    out_specs = (
        P(None, ("ctx", "head"), None),
        P(None, ("ctx", "head"), None),
        P(None, ("ctx", "head"), None),
        P("head"),
    )
    return jax.shard_map(local, mesh=mesh, in_specs=in_specs, out_specs=out_specs, check_vma=False)
```

```python
import functools
import math

import jax
import jax.numpy as jnp
from jax import lax
from jax.experimental import pallas as pl
from jax.experimental.pallas import tpu as pltpu
from jax.sharding import PartitionSpec as P

MESH = pl.DeviceIdType.MESH
F32, BF16 = jnp.float32, jnp.bfloat16
HG = 3
BLK = 64
NH = 4
ROWS = BLK // NH
W = 256
COLS = NH * HG * W
PLANE = 8
DEPTH = 16
EARLY = 4
SCALE = 1.0 / math.sqrt(128.0)


def nt(a, b):
    return lax.dot_general(a, b, (((1,), (1,)), ((), ())), preferred_element_type=F32)


def nn(a, b):
    return lax.dot_general(a, b, (((1,), (0,)), ((), ())), preferred_element_type=F32)


def tn(a, b):
    return lax.dot_general(a, b, (((0,), (0,)), ((), ())), preferred_element_type=F32)


def second_map(q1, do, k1, v, rows, mask):
    inner = nt(v, do)
    p1 = jnp.where(mask, jnp.exp(nt(k1, q1) * SCALE - rows[1]), 0.0)
    return p1, inner, jnp.sum(p1 * inner, axis=0, keepdims=True)


def gradients(p1, inner, q0, q1, do, k0, k1, rows, lam, mask):
    n0, _, d0, d1 = rows
    p0 = jnp.where(mask, jnp.exp(nt(k0, q0) * SCALE - n0), 0.0)
    mixed = (p0 - lam * p1).astype(BF16)
    g0 = (SCALE * p0 * (inner - d0)).astype(BF16)
    g1 = ((-lam * SCALE) * p1 * (inner - d1)).astype(BF16)
    dv = nn(mixed, do)
    dk = jnp.concatenate([nn(g0, q0), nn(g1, q1)], axis=1)
    dq = jnp.concatenate([tn(g0, k0), tn(g1, k1)], axis=1)
    return dq, dk, dv


def wait_for(ref, sem):
    pltpu.make_async_copy(ref, ref, sem).wait()


def rounded(x):
    return x.astype(BF16).reshape(2, BLK, W)


def main_kernel(
    n,
    q_hbm, k_hbm, v_hbm, do_hbm, norm_hbm, delta_hbm, lam_hbm,
    landed, back, lbuf2,
    lam_s, q_v, k_v, v_v, do_v, nv, dv_, nd, ndr, rnd, r_a, r_b, w_kv, h_qd, h_nd, r_p1, r_in,
    acc, stage, st_p, st_wkv, st_wq, wkv, wq, lam_tile, lbuf1,
    in_sem, own_sem, qs_send, a_recv, b_recv, f_send, nd_send, nd_recv, ws_send, w_recv,
    hs_send, h_recv, hn_recv, wq_send, wq_recv,
    r_send, r_recv, p_send, p_recv, pw_send, pw_recv, l_send, l_recv, line_sem,
):
    me = lax.axis_index("ctx")
    hd = lax.axis_index("head")
    z, r8 = me // PLANE, me % PLANE

    def ctx(d):
        return lax.rem(me + (d + n), n)

    def head(d):
        return lax.rem(hd + d, NH)

    def line(d):
        return lax.rem(z + d, DEPTH) * PLANE + r8

    def ahead(s):
        return me + s < n

    def behind(s):
        return me >= s

    last_two = me >= n - 2
    host = (me >= PLANE - 2) & (me < PLANE)
    guest = me + (n - PLANE)

    def hosts(s):
        return host & (me + s >= PLANE)

    loads = [
        pltpu.make_async_copy(a, b, in_sem.at[i])
        for i, (a, b) in enumerate(
            [(q_hbm, q_v), (do_hbm, do_v), (norm_hbm, nv), (delta_hbm, dv_), (k_hbm, k_v), (v_hbm, v_v), (lam_hbm, lam_s)]
        )
    ]
    for c in loads:
        c.start()

    barrier = pltpu.get_barrier_semaphore()

    def tell(c, h):
        pl.semaphore_signal(barrier, inc=1, device_id=(c, h), device_id_type=MESH)

    heads = range(NH)
    for s in (1, 2):

        @pl.when(behind(s))
        def _():
            for d in heads:
                tell(ctx(-s), head(d))

        @pl.when(ahead(s))
        def _():
            for d in heads:
                tell(ctx(s), head(d))

        @pl.when(~behind(s))
        def _():
            for d in heads:
                tell(me - s + PLANE, head(d))

    for d in range(1, PLANE):
        tell(z * PLANE + lax.rem(r8 + d, PLANE), hd)
    for d in range(1, NH):
        tell(me, head(d))

    @pl.when(z < EARLY)
    def _():
        for d in range(1, DEPTH):
            tell(line(d), hd)

    @pl.when(host)
    def _():
        for d in range(1, NH):
            tell(guest, head(d))

    def when(condition, count):
        return jnp.where(condition, count, 0)

    for c in loads:
        c.wait()
    for half in range(2):
        lanes = pl.ds(half * BLK, BLK)
        for i in range(HG):
            nd[2 * i : 2 * i + 2, lanes] = nv[half, i]
            nd[8 + 2 * i : 10 + 2 * i, lanes] = dv_[half, i]

    pl.semaphore_wait(
        barrier,
        sum(when(ahead(s), NH) + when(behind(s), NH) + when(hosts(s), NH) for s in (1, 2))
        + EARLY - when(z < EARLY, 1) + when(last_two, NH - 1) + (NH - 1) + (PLANE - 1),
    )

    @pl.when(z > 0)
    def _():
        pl.semaphore_signal(line_sem.at[0], inc=1, device_id=(r8, hd), device_id_type=MESH)

    @pl.when(last_two)
    def _():
        for d in heads:
            pl.semaphore_signal(line_sem.at[2], inc=1, device_id=(r8, head(d)), device_id_type=MESH)

    def map_cols(g, m):
        return pl.ds(g * W + m * 128, 128)

    def send_first(g, s):
        for i, (ref, cols, lanes) in enumerate(
            ((q_v, map_cols(g, 1), pl.ds(0, 128)), (do_v, pl.ds(g * W, W), pl.ds(128, W)))
        ):
            pltpu.make_async_remote_copy(
                src_ref=ref.at[1, :, cols], dst_ref=r_a.at[g, s - 1, :, lanes],
                send_sem=qs_send.at[s - 1, i], recv_sem=a_recv.at[s - 1, g],
                device_id=(ctx(s), hd), device_id_type=MESH,
            ).start()

    def send_second(g, s):
        pltpu.make_async_remote_copy(
            src_ref=q_v.at[1, :, map_cols(g, 0)], dst_ref=r_b.at[g, s - 1],
            send_sem=qs_send.at[s - 1, 2], recv_sem=b_recv.at[s - 1, g],
            device_id=(ctx(s), hd), device_id_type=MESH,
        ).start()

    def send_nd(dst, c, send, recv):
        pltpu.make_async_remote_copy(
            src_ref=nd, dst_ref=dst, send_sem=send, recv_sem=recv, device_id=(c, hd), device_id_type=MESH
        ).start()

    @pl.when(last_two)
    def _():
        send_nd(h_nd, r8, hs_send.at[2], hn_recv)
        for g in range(HG):
            for i, ref in enumerate((q_v, do_v)):
                pltpu.make_async_remote_copy(
                    src_ref=ref.at[:, :, pl.ds(g * W, W)], dst_ref=h_qd.at[g, :, :, pl.ds(i * W, W)],
                    send_sem=hs_send.at[i], recv_sem=h_recv.at[g],
                    device_id=(r8, hd), device_id_type=MESH,
                ).start()

    for s in (1, 2):

        @pl.when(ahead(s))
        def _():
            send_nd(rnd.at[s - 1], ctx(s), nd_send.at[s - 1], nd_recv.at[s - 1])

    odd = r8 % 2 == 1
    for g in range(HG):
        for s in (2, 1):

            @pl.when(ahead(s) & ~odd if g == 0 and s == 1 else ahead(s))
            def _():
                send_first(g, s)

    for s in (1, 2):

        @pl.when(~behind(s))
        def _():
            for g in range(HG):
                for i, ref in enumerate((k_v, v_v)):
                    pltpu.make_async_remote_copy(
                        src_ref=ref.at[0, :, pl.ds(g * W, W)], dst_ref=w_kv.at[g, s - 1, :, pl.ds(i * W, W)],
                        send_sem=ws_send.at[s - 1, i], recv_sem=w_recv.at[s - 1, g],
                        device_id=(me - s + PLANE, hd), device_id_type=MESH,
                    ).start()


    for s in (1, 2):

        @pl.when(~behind(s))
        def _():
            r_a[:, s - 1] = jnp.zeros((HG, BLK, 128 + W), BF16)
            r_b[:, s - 1] = jnp.zeros((HG, BLK, 128), BF16)
            rnd[s - 1] = jnp.zeros((16, 128), F32)

    @pl.when(me == PLANE - 2)
    def _():
        w_kv[:, 0] = jnp.zeros((HG, BLK, 2 * W), BF16)

    @pl.when(me == n - 1)
    def _():
        back[0] = jnp.zeros((ROWS, COLS), BF16)

    kk = lax.broadcasted_iota(jnp.int32, (128, 128), 0)
    qq = lax.broadcasted_iota(jnp.int32, (128, 128), 1)
    own_mask = ((kk < 64) & (qq >= 64)) | (((kk < 64) == (qq < 64)) & (kk <= qq))
    rem_mask = (kk < 64) | (qq < 64) | (me >= 2)
    rem_mask = rem_mask & (me >= jnp.where(qq < 64, 1, 2))
    wrap_mask = (kk >= 64) | (me == PLANE - 1)

    def rows_of(ref, g):
        return [ref[i : i + 1, :] for i in (2 * g, 2 * g + 1, 8 + 2 * g, 9 + 2 * g)]

    def own(ref, g):
        return ref[:, :, pl.ds(g * W, W)].reshape(2 * BLK, W)

    def own_map(ref, g, m):
        return ref[:, :, map_cols(g, m)].reshape(2 * BLK, 128)

    def first(ref, g):
        both = ref[g].reshape(2 * BLK, 128 + W)
        return both[:, :128], both[:, 128:]

    def second(ref, g):
        return ref[g].reshape(2 * BLK, 128)

    def pair(ref, g):
        both = ref[g].reshape(2 * BLK, 2 * W)
        return both[:, :128], both[:, 128:W], both[:, W:]

    def out_cols(g):
        return pl.ds(pl.multiple_of((hd * HG + g) * W, W), W)

    def rows_at(h):
        return pl.ds(pl.multiple_of(h * ROWS, ROWS), ROWS)

    def spread(g):
        for d in range(1, NH):
            pltpu.make_async_remote_copy(
                src_ref=stage.at[g, :, rows_at(head(d)), :], dst_ref=landed.at[:, :, out_cols(g)],
                send_sem=r_send.at[g], recv_sem=r_recv,
                device_id=(me, head(d)), device_id_type=MESH,
            ).start()
        pltpu.make_async_copy(
            stage.at[g, :, rows_at(hd), :], landed.at[:, :, out_cols(g)], own_sem
        ).start()
        pass

    lam_tile[...] = jnp.zeros((8, 128), F32)
    for g in range(HG):
        q0, q1, do = own_map(q_v, g, 0), own_map(q_v, g, 1), own(do_v, g)
        k0, k1, v = own_map(k_v, g, 0), own_map(k_v, g, 1), own(v_v, g)
        p1, inner, lam_row = second_map(q1, do, k1, v, rows_of(nd, g), own_mask)
        dq, dk, dv = gradients(p1, inner, q0, q1, do, k0, k1, rows_of(nd, g), lam_s[g], own_mask)
        stage[g, 0:2] = rounded(dq)
        acc[g, 0] = dk
        acc[g, 1] = dv
        lam_tile[g : g + 1, :] = lam_row

    sent = [q_v.at[0, :, pl.ds(0, c)] for c in (HG * 128, HG * W, (HG - 1) * 128, (HG - 1) * W)]
    relays = odd & behind(2)

    @pl.when(relays)
    def _():
        wait_for(r_a.at[0, 1], a_recv.at[1, 0])
        pltpu.make_async_remote_copy(
            src_ref=r_a.at[0, 1], dst_ref=r_a.at[0, 0], send_sem=f_send, recv_sem=a_recv.at[0, 0],
            device_id=(ctx(-1), hd), device_id_type=MESH,
        ).start()

    def send_rest():
        for s in (1, 2):

            @pl.when(ahead(s) & ~odd if s == 1 else ahead(s))
            def _():
                wait_for(sent[0], qs_send.at[s - 1, 0])
                wait_for(sent[1], qs_send.at[s - 1, 1])

            if s == 1:

                @pl.when(ahead(s) & odd)
                def _():
                    wait_for(sent[2], qs_send.at[0, 0])
                    wait_for(sent[3], qs_send.at[0, 1])

            @pl.when(ahead(s))
            def _():
                for g in range(HG):
                    send_second(g, s)

    @pl.when(z == 0)
    def _():
        send_rest()


    for s in (1, 2):

        @pl.when(behind(s))
        def _():
            wait_for(rnd.at[s - 1], nd_recv.at[s - 1])

    left = lax.broadcasted_iota(jnp.int32, (16, 128), 1) < BLK
    ndr[...] = jnp.where(left, pltpu.roll(rnd[0], BLK, 1), rnd[1])

    for g in range(HG):
        for s in (1, 2):

            @pl.when(behind(s) & ~relays if g == 0 and s == 2 else behind(s))
            def _():
                wait_for(r_a.at[g, s - 1], a_recv.at[s - 1, g])

        q1, do = first(r_a, g)
        r_p1[g], r_in[g], lam_row = second_map(q1, do, own_map(k_v, g, 1), own(v_v, g), rows_of(ndr, g), rem_mask)
        lam_tile[g : g + 1, :] += lam_row

    def sum_over_plane():
        lbuf1[r8] = lam_tile[...]
        for d in range(1, PLANE):
            pltpu.make_async_remote_copy(
                src_ref=lbuf1.at[r8], dst_ref=lbuf1.at[r8],
                send_sem=l_send.at[0], recv_sem=l_recv.at[0],
                device_id=(z * PLANE + lax.rem(r8 + d, PLANE), hd), device_id_type=MESH,
            ).start()
        pass

    def send_sum(to):
        @pl.when(z != to)
        def _():
            pltpu.make_async_remote_copy(
                src_ref=lbuf2.at[z], dst_ref=lbuf2.at[z],
                send_sem=l_send.at[1], recv_sem=l_recv.at[1],
                device_id=(to * PLANE + r8, hd), device_id_type=MESH,
            ).start()

        pass

    def sum_over_line():
        wait_for(lbuf1.at[pl.ds(0, PLANE - 1)], l_recv.at[0])
        total = lbuf1[0]
        for i in range(1, PLANE):
            total = total + lbuf1[i]
        lbuf2[z] = total
        for to in range(EARLY):
            send_sum(to)

    @pl.when(z > 0)
    def _():
        sum_over_plane()
        send_rest()
        sum_over_line()

    for g in range(HG):
        for s in (1, 2):

            @pl.when(behind(s))
            def _():
                wait_for(r_b.at[g, s - 1], b_recv.at[s - 1, g])

        q1, do = first(r_a, g)
        dq, dk, dv = gradients(
            r_p1[g], r_in[g], second(r_b, g), q1, do, own_map(k_v, g, 0), own_map(k_v, g, 1),
            rows_of(ndr, g), lam_s[g], rem_mask,
        )
        for s in (1, 2):
            st_p[s - 1, :, pl.ds(g * W, W)] = rounded(dq)[s - 1]
        stage[g, 2:4] = rounded(acc[g, 0] + dk)
        stage[g, 4:6] = rounded(acc[g, 1] + dv)
        spread(g)
    all_cols = pl.ds(pl.multiple_of(hd * HG * W, W), HG * W)
    for s in (1, 2):

        @pl.when(behind(s))
        def _():
            for d in heads:
                pltpu.make_async_remote_copy(
                    src_ref=st_p.at[s - 1, rows_at(head(d)), :], dst_ref=back.at[s - 1, :, all_cols],
                    send_sem=p_send.at[s - 1], recv_sem=p_recv.at[s - 1],
                    device_id=(ctx(-s), head(d)), device_id_type=MESH,
                ).start()


    @pl.when(host)
    def _():
        pl.semaphore_wait(line_sem.at[2], NH)
        wait_for(h_nd, hn_recv)
        for g in range(HG):
            for s in (1, 2):

                @pl.when(hosts(s))
                def _():
                    wait_for(w_kv.at[g, s - 1], w_recv.at[s - 1, g])

            wait_for(h_qd.at[g], h_recv.at[g])
            q0, q1, do = pair(h_qd, g)
            k0, k1, v = pair(w_kv, g)
            p1, inner, lam_row = second_map(q1, do, k1, v, rows_of(h_nd, g), wrap_mask)
            lam_tile[g : g + 1, :] += lam_row
            dq, dk, dv = gradients(p1, inner, q0, q1, do, k0, k1, rows_of(h_nd, g), lam_s[g], wrap_mask)
            st_wq[g] = rounded(dq)
            for s in (1, 2):
                st_wkv[g, s - 1, 0] = rounded(dk)[s - 1]
                st_wkv[g, s - 1, 1] = rounded(dv)[s - 1]
            for s in (1, 2):

                @pl.when(hosts(s))
                def _():
                    for d in heads:
                        pltpu.make_async_remote_copy(
                            src_ref=st_wkv.at[g, s - 1, :, rows_at(head(d)), :],
                            dst_ref=wkv.at[s - 1, :, :, out_cols(g)],
                            send_sem=pw_send.at[s - 1, g], recv_sem=pw_recv.at[s - 1],
                            device_id=(me + s - PLANE, head(d)), device_id_type=MESH,
                        ).start()

            for d in heads:
                pltpu.make_async_remote_copy(
                    src_ref=st_wq.at[g, :, rows_at(head(d)), :], dst_ref=wq.at[:, :, out_cols(g)],
                    send_sem=wq_send.at[g], recv_sem=wq_recv,
                    device_id=(guest, head(d)), device_id_type=MESH,
                ).start()

    @pl.when(z == 0)
    def _():
        sum_over_plane()

    @pl.when(z == 0)
    def _():
        pl.semaphore_wait(line_sem.at[0], DEPTH - 1)
        for d in range(1, DEPTH):
            pl.semaphore_signal(line_sem.at[1], inc=1, device_id=(line(d), hd), device_id_type=MESH)

    @pl.when(z == 0)
    def _():
        sum_over_line()

    @pl.when(z > 0)
    def _():
        pl.semaphore_wait(line_sem.at[1], 1)

    for to in range(EARLY, DEPTH):
        send_sum(to)

    wait_for(landed.at[:, :, pl.ds(0, (NH - 1) * HG * W)], r_recv)
    for g in range(HG):
        wait_for(stage.at[g, :, pl.ds(0, ROWS)], own_sem)
    for s in (1, 2):

        @pl.when(ahead(s))
        def _():
            wait_for(back.at[s - 1], p_recv.at[s - 1])

        @pl.when(~behind(s))
        def _():
            wait_for(wkv.at[s - 1], pw_recv.at[s - 1])

    @pl.when(me < 2)
    def _():
        for i in range(2):
            first_term = jnp.where(me == 0, wkv[0, i].astype(F32), 0.0)
            total = landed[2 + 2 * i].astype(F32) + first_term + wkv[1, i].astype(F32)
            landed[2 + 2 * i] = total.astype(BF16)

    @pl.when(last_two)
    def _():
        wait_for(wq, wq_recv)
        landed[0] = (landed[0].astype(F32) + wq[0].astype(F32)).astype(BF16)
        back[1] = wq[1]


    for s in (1, 2):

        @pl.when(ahead(s))
        def _():
            wait_for(sent[0], qs_send.at[s - 1, 2])
            wait_for(nd, nd_send.at[s - 1])
            pass

        @pl.when(~behind(s))
        def _():
            wait_for(sent[1], ws_send.at[s - 1, 0])
            wait_for(sent[1], ws_send.at[s - 1, 1])
            pass

        @pl.when(behind(s))
        def _():
            wait_for(st_p.at[s - 1], p_send.at[s - 1])

        @pl.when(hosts(s))
        def _():
            for g in range(HG):
                wait_for(st_wkv.at[g, s - 1], pw_send.at[s - 1, g])


    @pl.when(relays)
    def _():
        wait_for(r_a.at[0, 1], f_send)

    @pl.when(host)
    def _():
        for g in range(HG):
            wait_for(st_wq.at[g], wq_send.at[g])
        pass

    @pl.when(last_two)
    def _():
        wait_for(q_v, hs_send.at[0])
        wait_for(q_v, hs_send.at[1])
        wait_for(nd, hs_send.at[2])
        pass

    for g in range(HG):
        wait_for(stage.at[g, :, pl.ds(0, (NH - 1) * ROWS)], r_send.at[g])
    wait_for(lbuf1.at[pl.ds(0, PLANE - 1)], l_send.at[0])
    wait_for(lbuf2.at[pl.ds(0, DEPTH - 1)], l_recv.at[1])
    wait_for(lbuf2.at[pl.ds(0, DEPTH - 1)], l_send.at[1])


def finish_kernel(landed, back, lbuf2, oq, ok, ov, lam_out, sum_q, sems):
    copies = [
        pltpu.make_async_copy(landed.at[pl.ds(2, 2)], ok, sems.at[0]),
        pltpu.make_async_copy(landed.at[pl.ds(4, 2)], ov, sems.at[1]),
        pltpu.make_async_copy(landed.at[0], oq.at[0], sems.at[2]),
        pltpu.make_async_copy(sum_q, oq.at[1], sems.at[3]),
    ]
    for c in copies[:3]:
        c.start()
    sum_q[...] = (landed[1].astype(F32) + back[0].astype(F32) + back[1].astype(F32)).astype(BF16)
    copies[3].start()
    total = lbuf2[0]
    for i in range(1, DEPTH):
        total = total + lbuf2[i]
    for g in range(HG):
        lam_out[g] = -jnp.sum(total[g : g + 1, :])
    for c in copies:
        c.wait()


def local(query_rows, key_rows, value_rows, out_grad, log_norms, row_deltas, lambdas):
    n = lax.axis_size("ctx")
    hbm = pl.BlockSpec(memory_space=pl.ANY)
    vmem = pl.BlockSpec(memory_space=pltpu.VMEM)
    smem = pl.BlockSpec(memory_space=pltpu.SMEM)
    half = (2, BLK, HG * W)
    dma, regular = pltpu.SemaphoreType.DMA, pltpu.SemaphoreType.REGULAR
    args = (
        query_rows, key_rows, value_rows, out_grad,
        jnp.swapaxes(log_norms, 1, 2), jnp.swapaxes(row_deltas, 1, 2), lambdas,
    )
    landed, back, sums = pl.pallas_call(
        functools.partial(main_kernel, n),
        out_shape=(
            pltpu.VMEM((6, ROWS, COLS), BF16), pltpu.VMEM((2, ROWS, COLS), BF16),
            pltpu.VMEM((DEPTH, 8, 128), F32),
        ),
        in_specs=[hbm] * 7,
        out_specs=(vmem,) * 3,
        scratch_shapes=[
            pltpu.SMEM((HG,), F32),
            pltpu.VMEM(half, BF16), pltpu.VMEM(half, BF16), pltpu.VMEM(half, BF16), pltpu.VMEM(half, BF16),
            pltpu.VMEM((2, HG, 2, BLK), F32), pltpu.VMEM((2, HG, 2, BLK), F32),
            pltpu.VMEM((16, 128), F32), pltpu.VMEM((16, 128), F32), pltpu.VMEM((2, 16, 128), F32),
            *[pltpu.VMEM((HG, 2, BLK, c), BF16) for c in (128 + W, 128, 2 * W, 2 * W)],
            pltpu.VMEM((16, 128), F32),
            *[pltpu.VMEM((HG, 2 * BLK, 2 * BLK), F32) for _ in range(2)],
            pltpu.VMEM((HG, 2, 2 * BLK, W), F32), pltpu.VMEM((HG, 6, BLK, W), BF16),
            pltpu.VMEM((2, BLK, HG * W), BF16),
            pltpu.VMEM((HG, 2, 2, BLK, W), BF16), pltpu.VMEM((HG, 2, BLK, W), BF16),
            pltpu.VMEM((2, 2, ROWS, COLS), BF16), pltpu.VMEM((2, ROWS, COLS), BF16),
            pltpu.VMEM((8, 128), F32), pltpu.VMEM((PLANE, 8, 128), F32),
            dma((7,)), dma, dma((2, 3)), dma((2, HG)), dma((2, HG)), dma, dma((2,)), dma((2,)),
            dma((2, 2)), dma((2, HG)), dma((3,)), dma((HG,)), dma, dma((HG,)), dma,
            dma((HG,)), dma, dma((2,)), dma((2,)), dma((2, HG)), dma((2,)), dma((2,)), dma((2,)),
            regular((3,)),
        ],
        compiler_params=pltpu.CompilerParams(
            collective_id=0, has_side_effects=True, vmem_limit_bytes=24 * 1024 * 1024
        ),
        cost_estimate=pl.CostEstimate(flops=3 * 10**8, bytes_accessed=2 * 10**6, transcendentals=2 * 10**5),
        name="attention_backward",
    )(*[pltpu.with_memory_space_constraint(x, pltpu.HBM) for x in args])
    out = jax.ShapeDtypeStruct((2, ROWS, COLS), BF16)
    return pl.pallas_call(
        finish_kernel,
        out_shape=(out, out, out, jax.ShapeDtypeStruct((HG,), F32)),
        in_specs=[vmem] * 3,
        out_specs=(hbm, hbm, hbm, smem),
        scratch_shapes=[pltpu.VMEM((ROWS, COLS), BF16), dma((4,))],
        compiler_params=pltpu.CompilerParams(vmem_limit_bytes=16 * 1024 * 1024),
        name="write_outputs",
    )(*[pltpu.with_memory_space_constraint(x, pltpu.VMEM) for x in (landed, back, sums)])


def solution(mesh):
    in_specs = (
        P(None, "ctx", "head"),
        P(None, "ctx", "head"),
        P(None, "ctx", "head"),
        P(None, "ctx", "head"),
        P(None, None, "head", "ctx"),
        P(None, None, "head", "ctx"),
        P("head"),
    )
    out_specs = (
        P(None, ("ctx", "head"), None),
        P(None, ("ctx", "head"), None),
        P(None, ("ctx", "head"), None),
        P("head"),
    )
    return jax.shard_map(local, mesh=mesh, in_specs=in_specs, out_specs=out_specs, check_vma=False)
```

```python
import functools
import math

import jax
import jax.numpy as jnp
from jax import lax
from jax.experimental import pallas as pl
from jax.experimental.pallas import tpu as pltpu
from jax.sharding import PartitionSpec as P

MESH = pl.DeviceIdType.MESH
F32, BF16 = jnp.float32, jnp.bfloat16
HG = 3
BLK = 64
NH = 4
ROWS = BLK // NH
W = 256
COLS = NH * HG * W
PLANE = 8
DEPTH = 16
EARLY = 4
SCALE = 1.0 / math.sqrt(128.0)


def nt(a, b):
    return lax.dot_general(a, b, (((1,), (1,)), ((), ())), preferred_element_type=F32)


def nn(a, b):
    return lax.dot_general(a, b, (((1,), (0,)), ((), ())), preferred_element_type=F32)


def tn(a, b):
    return lax.dot_general(a, b, (((0,), (0,)), ((), ())), preferred_element_type=F32)


def second_map(q1, do, k1, v, rows, mask):
    inner = nt(v, do)
    p1 = jnp.where(mask, jnp.exp(nt(k1, q1) * SCALE - rows[1]), 0.0)
    return p1, inner, jnp.sum(p1 * inner, axis=0, keepdims=True)


def gradients(p1, inner, q0, q1, do, k0, k1, rows, lam, mask):
    n0, _, d0, d1 = rows
    p0 = jnp.where(mask, jnp.exp(nt(k0, q0) * SCALE - n0), 0.0)
    mixed = (p0 - lam * p1).astype(BF16)
    g0 = (SCALE * p0 * (inner - d0)).astype(BF16)
    g1 = ((-lam * SCALE) * p1 * (inner - d1)).astype(BF16)
    dv = nn(mixed, do)
    dk = jnp.concatenate([nn(g0, q0), nn(g1, q1)], axis=1)
    dq = jnp.concatenate([tn(g0, k0), tn(g1, k1)], axis=1)
    return dq, dk, dv


def wait_for(ref, sem):
    pltpu.make_async_copy(ref, ref, sem).wait()


def rounded(x):
    return x.astype(BF16).reshape(2, BLK, W)


def main_kernel(
    n,
    q_hbm, k_hbm, v_hbm, do_hbm, norm_hbm, delta_hbm, lam_hbm,
    landed, back, lbuf2,
    lam_s, q_v, k_v, v_v, do_v, nv, dv_, nd, ndr, rnd, r_a, r_b, w_kv, h_qd, h_nd, r_p1, r_in,
    acc, stage, st_p, st_wkv, st_wq, wkv, wq, lam_tile, lbuf1,
    in_sem, own_sem, qs_send, a_recv, b_recv, f_send, nd_send, nd_recv, ws_send, w_recv,
    hs_send, h_recv, hn_recv, wq_send, wq_recv,
    r_send, r_recv, p_send, p_recv, pw_send, pw_recv, l_send, l_recv, line_sem,
):
    me = lax.axis_index("ctx")
    hd = lax.axis_index("head")
    z, r8 = me // PLANE, me % PLANE

    def ctx(d):
        return lax.rem(me + (d + n), n)

    def head(d):
        return lax.rem(hd + d, NH)

    def line(d):
        return lax.rem(z + d, DEPTH) * PLANE + r8

    def ahead(s):
        return me + s < n

    def behind(s):
        return me >= s

    last_two = me >= n - 2
    host = (me >= PLANE - 2) & (me < PLANE)
    guest = me + (n - PLANE)

    def hosts(s):
        return host & (me + s >= PLANE)

    loads = [
        pltpu.make_async_copy(a, b, in_sem.at[i])
        for i, (a, b) in enumerate(
            [(q_hbm, q_v), (do_hbm, do_v), (norm_hbm, nv), (delta_hbm, dv_), (k_hbm, k_v), (v_hbm, v_v), (lam_hbm, lam_s)]
        )
    ]
    for c in loads:
        c.start()

    barrier = pltpu.get_barrier_semaphore()

    def tell(c, h):
        pl.semaphore_signal(barrier, inc=1, device_id=(c, h), device_id_type=MESH)

    heads = range(NH)
    for s in (1, 2):

        @pl.when(behind(s))
        def _():
            for d in heads:
                tell(ctx(-s), head(d))

        @pl.when(ahead(s))
        def _():
            for d in heads:
                tell(ctx(s), head(d))

        @pl.when(~behind(s))
        def _():
            for d in heads:
                tell(me - s + PLANE, head(d))

    for d in range(1, PLANE):
        tell(z * PLANE + lax.rem(r8 + d, PLANE), hd)
    for d in range(1, NH):
        tell(me, head(d))

    @pl.when(z < EARLY)
    def _():
        for d in range(1, DEPTH):
            tell(line(d), hd)

    @pl.when(host)
    def _():
        for d in range(1, NH):
            tell(guest, head(d))

    def when(condition, count):
        return jnp.where(condition, count, 0)

    pl.semaphore_wait(
        barrier,
        sum(when(ahead(s), NH) + when(behind(s), NH) + when(hosts(s), NH) for s in (1, 2))
        + EARLY - when(z < EARLY, 1) + when(last_two, NH - 1) + (NH - 1) + (PLANE - 1),
    )

    @pl.when(z > 0)
    def _():
        pl.semaphore_signal(line_sem.at[0], inc=1, device_id=(r8, hd), device_id_type=MESH)

    @pl.when(last_two)
    def _():
        for d in heads:
            pl.semaphore_signal(line_sem.at[2], inc=1, device_id=(r8, head(d)), device_id_type=MESH)

    def map_cols(g, m):
        return pl.ds(g * W + m * 128, 128)

    def send_first(g, s):
        for i, (ref, cols, lanes) in enumerate(
            ((q_v, map_cols(g, 1), pl.ds(0, 128)), (do_v, pl.ds(g * W, W), pl.ds(128, W)))
        ):
            pltpu.make_async_remote_copy(
                src_ref=ref.at[1, :, cols], dst_ref=r_a.at[g, s - 1, :, lanes],
                send_sem=qs_send.at[s - 1, i], recv_sem=a_recv.at[s - 1, g],
                device_id=(ctx(s), hd), device_id_type=MESH,
            ).start()

    def send_second(g, s):
        pltpu.make_async_remote_copy(
            src_ref=q_v.at[1, :, map_cols(g, 0)], dst_ref=r_b.at[g, s - 1],
            send_sem=qs_send.at[s - 1, 2], recv_sem=b_recv.at[s - 1, g],
            device_id=(ctx(s), hd), device_id_type=MESH,
        ).start()

    def send_nd(dst, c, send, recv):
        pltpu.make_async_remote_copy(
            src_ref=nd, dst_ref=dst, send_sem=send, recv_sem=recv, device_id=(c, hd), device_id_type=MESH
        ).start()

    for c in loads:
        c.wait()
    for half in range(2):
        lanes = pl.ds(half * BLK, BLK)
        for i in range(HG):
            nd[2 * i : 2 * i + 2, lanes] = nv[half, i]
            nd[8 + 2 * i : 10 + 2 * i, lanes] = dv_[half, i]

    @pl.when(last_two)
    def _():
        send_nd(h_nd, r8, hs_send.at[2], hn_recv)
        for g in range(HG):
            for i, ref in enumerate((q_v, do_v)):
                pltpu.make_async_remote_copy(
                    src_ref=ref.at[:, :, pl.ds(g * W, W)], dst_ref=h_qd.at[g, :, :, pl.ds(i * W, W)],
                    send_sem=hs_send.at[i], recv_sem=h_recv.at[g],
                    device_id=(r8, hd), device_id_type=MESH,
                ).start()

    for s in (1, 2):

        @pl.when(ahead(s))
        def _():
            send_nd(rnd.at[s - 1], ctx(s), nd_send.at[s - 1], nd_recv.at[s - 1])

    odd = r8 % 2 == 1
    for g in range(HG):
        for s in (2, 1):

            @pl.when(ahead(s) & ~odd if g == 0 and s == 1 else ahead(s))
            def _():
                send_first(g, s)

    for s in (1, 2):

        @pl.when(~behind(s))
        def _():
            for g in range(HG):
                for i, ref in enumerate((k_v, v_v)):
                    pltpu.make_async_remote_copy(
                        src_ref=ref.at[0, :, pl.ds(g * W, W)], dst_ref=w_kv.at[g, s - 1, :, pl.ds(i * W, W)],
                        send_sem=ws_send.at[s - 1, i], recv_sem=w_recv.at[s - 1, g],
                        device_id=(me - s + PLANE, hd), device_id_type=MESH,
                    ).start()


    for s in (1, 2):

        @pl.when(~behind(s))
        def _():
            r_a[:, s - 1] = jnp.zeros((HG, BLK, 128 + W), BF16)
            r_b[:, s - 1] = jnp.zeros((HG, BLK, 128), BF16)
            rnd[s - 1] = jnp.zeros((16, 128), F32)

    @pl.when(me == PLANE - 2)
    def _():
        w_kv[:, 0] = jnp.zeros((HG, BLK, 2 * W), BF16)

    @pl.when(me == n - 1)
    def _():
        back[0] = jnp.zeros((ROWS, COLS), BF16)

    kk = lax.broadcasted_iota(jnp.int32, (128, 128), 0)
    qq = lax.broadcasted_iota(jnp.int32, (128, 128), 1)
    own_mask = ((kk < 64) & (qq >= 64)) | (((kk < 64) == (qq < 64)) & (kk <= qq))
    rem_mask = (kk < 64) | (qq < 64) | (me >= 2)
    rem_mask = rem_mask & (me >= jnp.where(qq < 64, 1, 2))
    wrap_mask = (kk >= 64) | (me == PLANE - 1)

    def rows_of(ref, g):
        return [ref[i : i + 1, :] for i in (2 * g, 2 * g + 1, 8 + 2 * g, 9 + 2 * g)]

    def own(ref, g):
        return ref[:, :, pl.ds(g * W, W)].reshape(2 * BLK, W)

    def own_map(ref, g, m):
        return ref[:, :, map_cols(g, m)].reshape(2 * BLK, 128)

    def first(ref, g):
        both = ref[g].reshape(2 * BLK, 128 + W)
        return both[:, :128], both[:, 128:]

    def second(ref, g):
        return ref[g].reshape(2 * BLK, 128)

    def pair(ref, g):
        both = ref[g].reshape(2 * BLK, 2 * W)
        return both[:, :128], both[:, 128:W], both[:, W:]

    def out_cols(g):
        return pl.ds(pl.multiple_of((hd * HG + g) * W, W), W)

    def rows_at(h):
        return pl.ds(pl.multiple_of(h * ROWS, ROWS), ROWS)

    def spread(g):
        for d in range(1, NH):
            pltpu.make_async_remote_copy(
                src_ref=stage.at[g, :, rows_at(head(d)), :], dst_ref=landed.at[:, :, out_cols(g)],
                send_sem=r_send.at[g], recv_sem=r_recv,
                device_id=(me, head(d)), device_id_type=MESH,
            ).start()
        pltpu.make_async_copy(
            stage.at[g, :, rows_at(hd), :], landed.at[:, :, out_cols(g)], own_sem
        ).start()
        pass

    lam_tile[...] = jnp.zeros((8, 128), F32)
    for g in range(HG):
        q0, q1, do = own_map(q_v, g, 0), own_map(q_v, g, 1), own(do_v, g)
        k0, k1, v = own_map(k_v, g, 0), own_map(k_v, g, 1), own(v_v, g)
        p1, inner, lam_row = second_map(q1, do, k1, v, rows_of(nd, g), own_mask)
        dq, dk, dv = gradients(p1, inner, q0, q1, do, k0, k1, rows_of(nd, g), lam_s[g], own_mask)
        stage[g, 0:2] = rounded(dq)
        acc[g, 0] = dk
        acc[g, 1] = dv
        lam_tile[g : g + 1, :] = lam_row

    sent = [q_v.at[0, :, pl.ds(0, c)] for c in (HG * 128, HG * W, (HG - 1) * 128, (HG - 1) * W)]
    relays = odd & behind(2)

    @pl.when(relays)
    def _():
        wait_for(r_a.at[0, 1], a_recv.at[1, 0])
        pltpu.make_async_remote_copy(
            src_ref=r_a.at[0, 1], dst_ref=r_a.at[0, 0], send_sem=f_send, recv_sem=a_recv.at[0, 0],
            device_id=(ctx(-1), hd), device_id_type=MESH,
        ).start()

    for s in (1, 2):

        @pl.when(ahead(s) & ~odd if s == 1 else ahead(s))
        def _():
            wait_for(sent[0], qs_send.at[s - 1, 0])
            wait_for(sent[1], qs_send.at[s - 1, 1])

        if s == 1:

            @pl.when(ahead(s) & odd)
            def _():
                wait_for(sent[2], qs_send.at[0, 0])
                wait_for(sent[3], qs_send.at[0, 1])

        @pl.when(ahead(s))
        def _():
            for g in range(HG):
                send_second(g, s)


    for s in (1, 2):

        @pl.when(behind(s))
        def _():
            wait_for(rnd.at[s - 1], nd_recv.at[s - 1])

    left = lax.broadcasted_iota(jnp.int32, (16, 128), 1) < BLK
    ndr[...] = jnp.where(left, pltpu.roll(rnd[0], BLK, 1), rnd[1])

    for g in range(HG):
        for s in (1, 2):

            @pl.when(behind(s) & ~relays if g == 0 and s == 2 else behind(s))
            def _():
                wait_for(r_a.at[g, s - 1], a_recv.at[s - 1, g])

        q1, do = first(r_a, g)
        r_p1[g], r_in[g], lam_row = second_map(q1, do, own_map(k_v, g, 1), own(v_v, g), rows_of(ndr, g), rem_mask)
        lam_tile[g : g + 1, :] += lam_row

    def sum_over_plane():
        lbuf1[r8] = lam_tile[...]
        for d in range(1, PLANE):
            pltpu.make_async_remote_copy(
                src_ref=lbuf1.at[r8], dst_ref=lbuf1.at[r8],
                send_sem=l_send.at[0], recv_sem=l_recv.at[0],
                device_id=(z * PLANE + lax.rem(r8 + d, PLANE), hd), device_id_type=MESH,
            ).start()
        pass

    def sum_over_line():
        wait_for(lbuf1.at[pl.ds(0, PLANE - 1)], l_recv.at[0])
        total = lbuf1[0]
        for i in range(1, PLANE):
            total = total + lbuf1[i]
        lbuf2[z] = total

        def send_sum(to):
            @pl.when(z != to)
            def _():
                pltpu.make_async_remote_copy(
                    src_ref=lbuf2.at[z], dst_ref=lbuf2.at[z],
                    send_sem=l_send.at[1], recv_sem=l_recv.at[1],
                    device_id=(to * PLANE + r8, hd), device_id_type=MESH,
                ).start()

        for to in range(EARLY):
            send_sum(to)

        @pl.when(z > 0)
        def _():
            pl.semaphore_wait(line_sem.at[1], 1)

        for to in range(EARLY, DEPTH):
            send_sum(to)

    @pl.when(z > 0)
    def _():
        sum_over_plane()

    for g in range(HG):
        for s in (1, 2):

            @pl.when(behind(s))
            def _():
                wait_for(r_b.at[g, s - 1], b_recv.at[s - 1, g])

        q1, do = first(r_a, g)
        dq, dk, dv = gradients(
            r_p1[g], r_in[g], second(r_b, g), q1, do, own_map(k_v, g, 0), own_map(k_v, g, 1),
            rows_of(ndr, g), lam_s[g], rem_mask,
        )
        for s in (1, 2):
            st_p[s - 1, :, pl.ds(g * W, W)] = rounded(dq)[s - 1]
        stage[g, 2:4] = rounded(acc[g, 0] + dk)
        stage[g, 4:6] = rounded(acc[g, 1] + dv)
        spread(g)
        if g == 1:

            @pl.when(z > 0)
            def _():
                sum_over_line()

    all_cols = pl.ds(pl.multiple_of(hd * HG * W, W), HG * W)
    for s in (1, 2):

        @pl.when(behind(s))
        def _():
            for d in heads:
                pltpu.make_async_remote_copy(
                    src_ref=st_p.at[s - 1, rows_at(head(d)), :], dst_ref=back.at[s - 1, :, all_cols],
                    send_sem=p_send.at[s - 1], recv_sem=p_recv.at[s - 1],
                    device_id=(ctx(-s), head(d)), device_id_type=MESH,
                ).start()


    @pl.when(host)
    def _():
        pl.semaphore_wait(line_sem.at[2], NH)
        wait_for(h_nd, hn_recv)
        for g in range(HG):
            for s in (1, 2):

                @pl.when(hosts(s))
                def _():
                    wait_for(w_kv.at[g, s - 1], w_recv.at[s - 1, g])

            wait_for(h_qd.at[g], h_recv.at[g])
            q0, q1, do = pair(h_qd, g)
            k0, k1, v = pair(w_kv, g)
            p1, inner, lam_row = second_map(q1, do, k1, v, rows_of(h_nd, g), wrap_mask)
            lam_tile[g : g + 1, :] += lam_row
            dq, dk, dv = gradients(p1, inner, q0, q1, do, k0, k1, rows_of(h_nd, g), lam_s[g], wrap_mask)
            st_wq[g] = rounded(dq)
            for s in (1, 2):
                st_wkv[g, s - 1, 0] = rounded(dk)[s - 1]
                st_wkv[g, s - 1, 1] = rounded(dv)[s - 1]
            for s in (1, 2):

                @pl.when(hosts(s))
                def _():
                    for d in heads:
                        pltpu.make_async_remote_copy(
                            src_ref=st_wkv.at[g, s - 1, :, rows_at(head(d)), :],
                            dst_ref=wkv.at[s - 1, :, :, out_cols(g)],
                            send_sem=pw_send.at[s - 1, g], recv_sem=pw_recv.at[s - 1],
                            device_id=(me + s - PLANE, head(d)), device_id_type=MESH,
                        ).start()

            for d in heads:
                pltpu.make_async_remote_copy(
                    src_ref=st_wq.at[g, :, rows_at(head(d)), :], dst_ref=wq.at[:, :, out_cols(g)],
                    send_sem=wq_send.at[g], recv_sem=wq_recv,
                    device_id=(guest, head(d)), device_id_type=MESH,
                ).start()

    @pl.when(z == 0)
    def _():
        sum_over_plane()

    @pl.when(z == 0)
    def _():
        pl.semaphore_wait(line_sem.at[0], DEPTH - 1)
        for d in range(1, DEPTH):
            pl.semaphore_signal(line_sem.at[1], inc=1, device_id=(line(d), hd), device_id_type=MESH)

    @pl.when(z == 0)
    def _():
        sum_over_line()

    wait_for(landed.at[:, :, pl.ds(0, (NH - 1) * HG * W)], r_recv)
    for g in range(HG):
        wait_for(stage.at[g, :, pl.ds(0, ROWS)], own_sem)
    for s in (1, 2):

        @pl.when(ahead(s))
        def _():
            wait_for(back.at[s - 1], p_recv.at[s - 1])

        @pl.when(~behind(s))
        def _():
            wait_for(wkv.at[s - 1], pw_recv.at[s - 1])

    @pl.when(me < 2)
    def _():
        for i in range(2):
            first_term = jnp.where(me == 0, wkv[0, i].astype(F32), 0.0)
            total = landed[2 + 2 * i].astype(F32) + first_term + wkv[1, i].astype(F32)
            landed[2 + 2 * i] = total.astype(BF16)

    @pl.when(last_two)
    def _():
        wait_for(wq, wq_recv)
        landed[0] = (landed[0].astype(F32) + wq[0].astype(F32)).astype(BF16)
        back[1] = wq[1]


    for s in (1, 2):

        @pl.when(ahead(s))
        def _():
            wait_for(sent[0], qs_send.at[s - 1, 2])
            wait_for(nd, nd_send.at[s - 1])
            pass

        @pl.when(~behind(s))
        def _():
            wait_for(sent[1], ws_send.at[s - 1, 0])
            wait_for(sent[1], ws_send.at[s - 1, 1])
            pass

        @pl.when(behind(s))
        def _():
            wait_for(st_p.at[s - 1], p_send.at[s - 1])

        @pl.when(hosts(s))
        def _():
            for g in range(HG):
                wait_for(st_wkv.at[g, s - 1], pw_send.at[s - 1, g])


    @pl.when(relays)
    def _():
        wait_for(r_a.at[0, 1], f_send)

    @pl.when(host)
    def _():
        for g in range(HG):
            wait_for(st_wq.at[g], wq_send.at[g])
        pass

    @pl.when(last_two)
    def _():
        wait_for(q_v, hs_send.at[0])
        wait_for(q_v, hs_send.at[1])
        wait_for(nd, hs_send.at[2])
        pass

    for g in range(HG):
        wait_for(stage.at[g, :, pl.ds(0, (NH - 1) * ROWS)], r_send.at[g])
    wait_for(lbuf1.at[pl.ds(0, PLANE - 1)], l_send.at[0])
    wait_for(lbuf2.at[pl.ds(0, DEPTH - 1)], l_recv.at[1])
    wait_for(lbuf2.at[pl.ds(0, DEPTH - 1)], l_send.at[1])


def finish_kernel(landed, back, lbuf2, oq, ok, ov, lam_out, sum_q, sums, sems):
    copies = [
        pltpu.make_async_copy(landed.at[pl.ds(2, 2)], ok, sems.at[0]),
        pltpu.make_async_copy(landed.at[pl.ds(4, 2)], ov, sems.at[1]),
        pltpu.make_async_copy(landed.at[0], oq.at[0], sems.at[2]),
        pltpu.make_async_copy(sum_q, oq.at[1], sems.at[3]),
        pltpu.make_async_copy(sums, lam_out, sems.at[4]),
    ]
    for c in copies[:3]:
        c.start()
    sum_q[...] = (landed[1].astype(F32) + back[0].astype(F32) + back[1].astype(F32)).astype(BF16)
    copies[3].start()
    total = lbuf2[0]
    for i in range(1, DEPTH):
        total = total + lbuf2[i]
    for g in range(HG):
        sums[g] = -jnp.sum(total[g : g + 1, :])
    copies[4].start()
    for c in copies:
        c.wait()


def local(query_rows, key_rows, value_rows, out_grad, log_norms, row_deltas, lambdas):
    n = lax.axis_size("ctx")
    hbm = pl.BlockSpec(memory_space=pl.ANY)
    vmem = pl.BlockSpec(memory_space=pltpu.VMEM)
    half = (2, BLK, HG * W)
    dma, regular = pltpu.SemaphoreType.DMA, pltpu.SemaphoreType.REGULAR
    args = (
        query_rows, key_rows, value_rows, out_grad,
        jnp.swapaxes(log_norms, 1, 2), jnp.swapaxes(row_deltas, 1, 2), lambdas,
    )
    landed, back, sums = pl.pallas_call(
        functools.partial(main_kernel, n),
        out_shape=(
            pltpu.VMEM((6, ROWS, COLS), BF16), pltpu.VMEM((2, ROWS, COLS), BF16),
            pltpu.VMEM((DEPTH, 8, 128), F32),
        ),
        in_specs=[hbm] * 7,
        out_specs=(vmem,) * 3,
        scratch_shapes=[
            pltpu.SMEM((HG,), F32),
            pltpu.VMEM(half, BF16), pltpu.VMEM(half, BF16), pltpu.VMEM(half, BF16), pltpu.VMEM(half, BF16),
            pltpu.VMEM((2, HG, 2, BLK), F32), pltpu.VMEM((2, HG, 2, BLK), F32),
            pltpu.VMEM((16, 128), F32), pltpu.VMEM((16, 128), F32), pltpu.VMEM((2, 16, 128), F32),
            *[pltpu.VMEM((HG, 2, BLK, c), BF16) for c in (128 + W, 128, 2 * W, 2 * W)],
            pltpu.VMEM((16, 128), F32),
            *[pltpu.VMEM((HG, 2 * BLK, 2 * BLK), F32) for _ in range(2)],
            pltpu.VMEM((HG, 2, 2 * BLK, W), F32), pltpu.VMEM((HG, 6, BLK, W), BF16),
            pltpu.VMEM((2, BLK, HG * W), BF16),
            pltpu.VMEM((HG, 2, 2, BLK, W), BF16), pltpu.VMEM((HG, 2, BLK, W), BF16),
            pltpu.VMEM((2, 2, ROWS, COLS), BF16), pltpu.VMEM((2, ROWS, COLS), BF16),
            pltpu.VMEM((8, 128), F32), pltpu.VMEM((PLANE, 8, 128), F32),
            dma((7,)), dma, dma((2, 3)), dma((2, HG)), dma((2, HG)), dma, dma((2,)), dma((2,)),
            dma((2, 2)), dma((2, HG)), dma((3,)), dma((HG,)), dma, dma((HG,)), dma,
            dma((HG,)), dma, dma((2,)), dma((2,)), dma((2, HG)), dma((2,)), dma((2,)), dma((2,)),
            regular((3,)),
        ],
        compiler_params=pltpu.CompilerParams(
            collective_id=0, has_side_effects=True, vmem_limit_bytes=24 * 1024 * 1024
        ),
        cost_estimate=pl.CostEstimate(flops=3 * 10**8, bytes_accessed=2 * 10**6, transcendentals=2 * 10**5),
        name="attention_backward",
    )(*[pltpu.with_memory_space_constraint(x, pltpu.HBM) for x in args])
    out = jax.ShapeDtypeStruct((2, ROWS, COLS), BF16)
    return pl.pallas_call(
        finish_kernel,
        out_shape=(out, out, out, jax.ShapeDtypeStruct((HG,), F32)),
        in_specs=[vmem] * 3,
        out_specs=(hbm,) * 4,
        scratch_shapes=[pltpu.VMEM((ROWS, COLS), BF16), pltpu.SMEM((HG,), F32), dma((5,))],
        compiler_params=pltpu.CompilerParams(vmem_limit_bytes=16 * 1024 * 1024),
        name="write_outputs",
    )(*[pltpu.with_memory_space_constraint(x, pltpu.VMEM) for x in (landed, back, sums)])


def solution(mesh):
    in_specs = (
        P(None, "ctx", "head"),
        P(None, "ctx", "head"),
        P(None, "ctx", "head"),
        P(None, "ctx", "head"),
        P(None, None, "head", "ctx"),
        P(None, None, "head", "ctx"),
        P("head"),
    )
    out_specs = (
        P(None, ("ctx", "head"), None),
        P(None, ("ctx", "head"), None),
        P(None, ("ctx", "head"), None),
        P("head"),
    )
    return jax.shard_map(local, mesh=mesh, in_specs=in_specs, out_specs=out_specs, check_vma=False)
```

```python
import functools
import math

import jax
import jax.numpy as jnp
from jax import lax
from jax.experimental import pallas as pl
from jax.experimental.pallas import tpu as pltpu
from jax.sharding import PartitionSpec as P

MESH = pl.DeviceIdType.MESH
F32, BF16 = jnp.float32, jnp.bfloat16
HG = 3
BLK = 64
NH = 4
ROWS = BLK // NH
W = 256
COLS = NH * HG * W
PLANE = 8
DEPTH = 16
EARLY = 4
SCALE = 1.0 / math.sqrt(128.0)


def nt(a, b):
    return lax.dot_general(a, b, (((1,), (1,)), ((), ())), preferred_element_type=F32)


def nn(a, b):
    return lax.dot_general(a, b, (((1,), (0,)), ((), ())), preferred_element_type=F32)


def tn(a, b):
    return lax.dot_general(a, b, (((0,), (0,)), ((), ())), preferred_element_type=F32)


def second_map(q1, do, k1, v, rows, mask):
    inner = nt(v, do)
    p1 = jnp.where(mask, jnp.exp(nt(k1, q1) * SCALE - rows[1]), 0.0)
    return p1, inner, jnp.sum(p1 * inner, axis=0, keepdims=True)


def gradients(p1, inner, q0, q1, do, k0, k1, rows, lam, mask):
    n0, _, d0, d1 = rows
    p0 = jnp.where(mask, jnp.exp(nt(k0, q0) * SCALE - n0), 0.0)
    mixed = (p0 - lam * p1).astype(BF16)
    g0 = (SCALE * p0 * (inner - d0)).astype(BF16)
    g1 = ((-lam * SCALE) * p1 * (inner - d1)).astype(BF16)
    dv = nn(mixed, do)
    dk = jnp.concatenate([nn(g0, q0), nn(g1, q1)], axis=1)
    dq = jnp.concatenate([tn(g0, k0), tn(g1, k1)], axis=1)
    return dq, dk, dv


def wait_for(ref, sem):
    pltpu.make_async_copy(ref, ref, sem).wait()


def rounded(x):
    return x.astype(BF16).reshape(2, BLK, W)


def main_kernel(
    n,
    q_hbm, k_hbm, v_hbm, do_hbm, norm_hbm, delta_hbm, lam_hbm,
    landed, back, lbuf2,
    lam_s, q_v, k_v, v_v, do_v, nv, dv_, nd, ndr, rnd, r_a, r_b, w_kv, h_qd, h_nd, r_p1, r_in,
    acc, stage, st_p, st_wkv, st_wq, wkv, wq, lam_tile, lbuf1,
    in_sem, own_sem, qs_send, a_recv, b_recv, f_send, nd_send, nd_recv, ws_send, w_recv,
    hs_send, h_recv, hn_recv, wq_send, wq_recv,
    r_send, r_recv, p_send, p_recv, pw_send, pw_recv, l_send, l_recv, line_sem,
):
    me = lax.axis_index("ctx")
    hd = lax.axis_index("head")
    z, r8 = me // PLANE, me % PLANE

    def ctx(d):
        return lax.rem(me + (d + n), n)

    def head(d):
        return lax.rem(hd + d, NH)

    def line(d):
        return lax.rem(z + d, DEPTH) * PLANE + r8

    def ahead(s):
        return me + s < n

    def behind(s):
        return me >= s

    last_two = me >= n - 2
    host = (me >= PLANE - 2) & (me < PLANE)
    guest = me + (n - PLANE)

    def hosts(s):
        return host & (me + s >= PLANE)

    loads = [
        pltpu.make_async_copy(a, b, in_sem.at[i])
        for i, (a, b) in enumerate(
            [(q_hbm, q_v), (do_hbm, do_v), (norm_hbm, nv), (delta_hbm, dv_), (k_hbm, k_v), (v_hbm, v_v), (lam_hbm, lam_s)]
        )
    ]
    for c in loads:
        c.start()

    barrier = pltpu.get_barrier_semaphore()

    def tell(c, h):
        pl.semaphore_signal(barrier, inc=1, device_id=(c, h), device_id_type=MESH)

    heads = range(NH)
    for s in (1, 2):

        @pl.when(behind(s))
        def _():
            tell(ctx(-s), hd)

        @pl.when(ahead(s))
        def _():
            for d in heads:
                tell(ctx(s), head(d))

        @pl.when(~behind(s))
        def _():
            for d in heads:
                tell(me - s + PLANE, head(d))

    for d in range(1, PLANE):
        tell(z * PLANE + lax.rem(r8 + d, PLANE), hd)
    for d in range(1, NH):
        tell(me, head(d))

    @pl.when(z < EARLY)
    def _():
        for d in range(1, DEPTH):
            tell(line(d), hd)

    @pl.when(host)
    def _():
        for d in range(1, NH):
            tell(guest, head(d))

    def when(condition, count):
        return jnp.where(condition, count, 0)

    pl.semaphore_wait(
        barrier,
        sum(when(ahead(s), 1) + when(behind(s), NH) + when(hosts(s), NH) for s in (1, 2))
        + EARLY - when(z < EARLY, 1) + when(last_two, NH - 1) + (NH - 1) + (PLANE - 1),
    )

    @pl.when(z > 0)
    def _():
        pl.semaphore_signal(line_sem.at[0], inc=1, device_id=(r8, hd), device_id_type=MESH)

    @pl.when(last_two)
    def _():
        for d in heads:
            pl.semaphore_signal(line_sem.at[2], inc=1, device_id=(r8, head(d)), device_id_type=MESH)

    def map_cols(g, m):
        return pl.ds(g * W + m * 128, 128)

    def send_first(g, s):
        for i, (ref, cols, lanes) in enumerate(
            ((q_v, map_cols(g, 1), pl.ds(0, 128)), (do_v, pl.ds(g * W, W), pl.ds(128, W)))
        ):
            pltpu.make_async_remote_copy(
                src_ref=ref.at[1, :, cols], dst_ref=r_a.at[g, s - 1, :, lanes],
                send_sem=qs_send.at[s - 1, i], recv_sem=a_recv.at[s - 1, g],
                device_id=(ctx(s), hd), device_id_type=MESH,
            ).start()

    def send_second(g, s):
        pltpu.make_async_remote_copy(
            src_ref=q_v.at[1, :, map_cols(g, 0)], dst_ref=r_b.at[g, s - 1],
            send_sem=qs_send.at[s - 1, 2], recv_sem=b_recv.at[s - 1, g],
            device_id=(ctx(s), hd), device_id_type=MESH,
        ).start()

    def send_nd(dst, c, send, recv):
        pltpu.make_async_remote_copy(
            src_ref=nd, dst_ref=dst, send_sem=send, recv_sem=recv, device_id=(c, hd), device_id_type=MESH
        ).start()

    for c in loads:
        c.wait()
    for half in range(2):
        lanes = pl.ds(half * BLK, BLK)
        for i in range(HG):
            nd[2 * i : 2 * i + 2, lanes] = nv[half, i]
            nd[8 + 2 * i : 10 + 2 * i, lanes] = dv_[half, i]

    @pl.when(last_two)
    def _():
        send_nd(h_nd, r8, hs_send.at[2], hn_recv)
        for g in range(HG):
            for i, ref in enumerate((q_v, do_v)):
                pltpu.make_async_remote_copy(
                    src_ref=ref.at[:, :, pl.ds(g * W, W)], dst_ref=h_qd.at[g, :, :, pl.ds(i * W, W)],
                    send_sem=hs_send.at[i], recv_sem=h_recv.at[g],
                    device_id=(r8, hd), device_id_type=MESH,
                ).start()

    for s in (1, 2):

        @pl.when(ahead(s))
        def _():
            send_nd(rnd.at[s - 1], ctx(s), nd_send.at[s - 1], nd_recv.at[s - 1])

    odd = r8 % 2 == 1
    for g in range(HG):
        for s in (2, 1):

            @pl.when(ahead(s) & ~odd if g == 0 and s == 1 else ahead(s))
            def _():
                send_first(g, s)

    for s in (1, 2):

        @pl.when(~behind(s))
        def _():
            for g in range(HG):
                for i, ref in enumerate((k_v, v_v)):
                    pltpu.make_async_remote_copy(
                        src_ref=ref.at[0, :, pl.ds(g * W, W)], dst_ref=w_kv.at[g, s - 1, :, pl.ds(i * W, W)],
                        send_sem=ws_send.at[s - 1, i], recv_sem=w_recv.at[s - 1, g],
                        device_id=(me - s + PLANE, hd), device_id_type=MESH,
                    ).start()


    for s in (1, 2):

        @pl.when(~behind(s))
        def _():
            r_a[:, s - 1] = jnp.zeros((HG, BLK, 128 + W), BF16)
            r_b[:, s - 1] = jnp.zeros((HG, BLK, 128), BF16)
            rnd[s - 1] = jnp.zeros((16, 128), F32)

    @pl.when(me == PLANE - 2)
    def _():
        w_kv[:, 0] = jnp.zeros((HG, BLK, 2 * W), BF16)

    @pl.when(me == n - 1)
    def _():
        back[0] = jnp.zeros((ROWS, COLS), BF16)

    kk = lax.broadcasted_iota(jnp.int32, (128, 128), 0)
    qq = lax.broadcasted_iota(jnp.int32, (128, 128), 1)
    own_mask = ((kk < 64) & (qq >= 64)) | (((kk < 64) == (qq < 64)) & (kk <= qq))
    rem_mask = (kk < 64) | (qq < 64) | (me >= 2)
    rem_mask = rem_mask & (me >= jnp.where(qq < 64, 1, 2))
    wrap_mask = (kk >= 64) | (me == PLANE - 1)

    def rows_of(ref, g):
        return [ref[i : i + 1, :] for i in (2 * g, 2 * g + 1, 8 + 2 * g, 9 + 2 * g)]

    def own(ref, g):
        return ref[:, :, pl.ds(g * W, W)].reshape(2 * BLK, W)

    def own_map(ref, g, m):
        return ref[:, :, map_cols(g, m)].reshape(2 * BLK, 128)

    def first(ref, g):
        both = ref[g].reshape(2 * BLK, 128 + W)
        return both[:, :128], both[:, 128:]

    def second(ref, g):
        return ref[g].reshape(2 * BLK, 128)

    def pair(ref, g):
        both = ref[g].reshape(2 * BLK, 2 * W)
        return both[:, :128], both[:, 128:W], both[:, W:]

    def out_cols(g):
        return pl.ds(pl.multiple_of((hd * HG + g) * W, W), W)

    def rows_at(h):
        return pl.ds(pl.multiple_of(h * ROWS, ROWS), ROWS)

    def spread(g):
        for d in range(1, NH):
            pltpu.make_async_remote_copy(
                src_ref=stage.at[g, :, rows_at(head(d)), :], dst_ref=landed.at[:, :, out_cols(g)],
                send_sem=r_send.at[g], recv_sem=r_recv,
                device_id=(me, head(d)), device_id_type=MESH,
            ).start()
        pltpu.make_async_copy(
            stage.at[g, :, rows_at(hd), :], landed.at[:, :, out_cols(g)], own_sem
        ).start()
        pass

    lam_tile[...] = jnp.zeros((8, 128), F32)
    for g in range(HG):
        q0, q1, do = own_map(q_v, g, 0), own_map(q_v, g, 1), own(do_v, g)
        k0, k1, v = own_map(k_v, g, 0), own_map(k_v, g, 1), own(v_v, g)
        p1, inner, lam_row = second_map(q1, do, k1, v, rows_of(nd, g), own_mask)
        dq, dk, dv = gradients(p1, inner, q0, q1, do, k0, k1, rows_of(nd, g), lam_s[g], own_mask)
        stage[g, 0:2] = rounded(dq)
        acc[g, 0] = dk
        acc[g, 1] = dv
        lam_tile[g : g + 1, :] = lam_row

    sent = [q_v.at[0, :, pl.ds(0, c)] for c in (HG * 128, HG * W, (HG - 1) * 128, (HG - 1) * W)]
    relays = odd & behind(2)

    @pl.when(relays)
    def _():
        wait_for(r_a.at[0, 1], a_recv.at[1, 0])
        pltpu.make_async_remote_copy(
            src_ref=r_a.at[0, 1], dst_ref=r_a.at[0, 0], send_sem=f_send, recv_sem=a_recv.at[0, 0],
            device_id=(ctx(-1), hd), device_id_type=MESH,
        ).start()

    for s in (1, 2):

        @pl.when(ahead(s) & ~odd if s == 1 else ahead(s))
        def _():
            wait_for(sent[0], qs_send.at[s - 1, 0])
            wait_for(sent[1], qs_send.at[s - 1, 1])

        if s == 1:

            @pl.when(ahead(s) & odd)
            def _():
                wait_for(sent[2], qs_send.at[0, 0])
                wait_for(sent[3], qs_send.at[0, 1])

        @pl.when(ahead(s))
        def _():
            for g in range(HG):
                send_second(g, s)


    for s in (1, 2):

        @pl.when(behind(s))
        def _():
            wait_for(rnd.at[s - 1], nd_recv.at[s - 1])

    left = lax.broadcasted_iota(jnp.int32, (16, 128), 1) < BLK
    ndr[...] = jnp.where(left, pltpu.roll(rnd[0], BLK, 1), rnd[1])

    for g in range(HG):
        for s in (1, 2):

            @pl.when(behind(s) & ~relays if g == 0 and s == 2 else behind(s))
            def _():
                wait_for(r_a.at[g, s - 1], a_recv.at[s - 1, g])

        q1, do = first(r_a, g)
        r_p1[g], r_in[g], lam_row = second_map(q1, do, own_map(k_v, g, 1), own(v_v, g), rows_of(ndr, g), rem_mask)
        lam_tile[g : g + 1, :] += lam_row

    def sum_over_plane():
        lbuf1[r8] = lam_tile[...]
        for d in range(1, PLANE):
            pltpu.make_async_remote_copy(
                src_ref=lbuf1.at[r8], dst_ref=lbuf1.at[r8],
                send_sem=l_send.at[0], recv_sem=l_recv.at[0],
                device_id=(z * PLANE + lax.rem(r8 + d, PLANE), hd), device_id_type=MESH,
            ).start()
        pass

    def sum_over_line():
        wait_for(lbuf1.at[pl.ds(0, PLANE - 1)], l_recv.at[0])
        total = lbuf1[0]
        for i in range(1, PLANE):
            total = total + lbuf1[i]
        lbuf2[z] = total

        def send_sum(to):
            @pl.when(z != to)
            def _():
                pltpu.make_async_remote_copy(
                    src_ref=lbuf2.at[z], dst_ref=lbuf2.at[z],
                    send_sem=l_send.at[1], recv_sem=l_recv.at[1],
                    device_id=(to * PLANE + r8, hd), device_id_type=MESH,
                ).start()

        for to in range(EARLY):
            send_sum(to)

        @pl.when(z > 0)
        def _():
            pl.semaphore_wait(line_sem.at[1], 1)

        for to in range(EARLY, DEPTH):
            send_sum(to)

    @pl.when(z > 0)
    def _():
        sum_over_plane()

    for g in range(HG):
        for s in (1, 2):

            @pl.when(behind(s))
            def _():
                wait_for(r_b.at[g, s - 1], b_recv.at[s - 1, g])

        q1, do = first(r_a, g)
        dq, dk, dv = gradients(
            r_p1[g], r_in[g], second(r_b, g), q1, do, own_map(k_v, g, 0), own_map(k_v, g, 1),
            rows_of(ndr, g), lam_s[g], rem_mask,
        )
        for s in (1, 2):
            st_p[s - 1, :, pl.ds(g * W, W)] = rounded(dq)[s - 1]
        stage[g, 2:4] = rounded(acc[g, 0] + dk)
        stage[g, 4:6] = rounded(acc[g, 1] + dv)
        spread(g)
        if g == 1:

            @pl.when(z > 0)
            def _():
                sum_over_line()

    all_cols = pl.ds(pl.multiple_of(hd * HG * W, W), HG * W)
    for s in (1, 2):

        @pl.when(behind(s))
        def _():
            for d in heads:
                pltpu.make_async_remote_copy(
                    src_ref=st_p.at[s - 1, rows_at(head(d)), :], dst_ref=back.at[s - 1, :, all_cols],
                    send_sem=p_send.at[s - 1], recv_sem=p_recv.at[s - 1],
                    device_id=(ctx(-s), head(d)), device_id_type=MESH,
                ).start()


    @pl.when(host)
    def _():
        pl.semaphore_wait(line_sem.at[2], NH)
        wait_for(h_nd, hn_recv)
        for g in range(HG):
            for s in (1, 2):

                @pl.when(hosts(s))
                def _():
                    wait_for(w_kv.at[g, s - 1], w_recv.at[s - 1, g])

            wait_for(h_qd.at[g], h_recv.at[g])
            q0, q1, do = pair(h_qd, g)
            k0, k1, v = pair(w_kv, g)
            p1, inner, lam_row = second_map(q1, do, k1, v, rows_of(h_nd, g), wrap_mask)
            lam_tile[g : g + 1, :] += lam_row
            dq, dk, dv = gradients(p1, inner, q0, q1, do, k0, k1, rows_of(h_nd, g), lam_s[g], wrap_mask)
            st_wq[g] = rounded(dq)
            for s in (1, 2):
                st_wkv[g, s - 1, 0] = rounded(dk)[s - 1]
                st_wkv[g, s - 1, 1] = rounded(dv)[s - 1]
            for s in (1, 2):

                @pl.when(hosts(s))
                def _():
                    for d in heads:
                        pltpu.make_async_remote_copy(
                            src_ref=st_wkv.at[g, s - 1, :, rows_at(head(d)), :],
                            dst_ref=wkv.at[s - 1, :, :, out_cols(g)],
                            send_sem=pw_send.at[s - 1, g], recv_sem=pw_recv.at[s - 1],
                            device_id=(me + s - PLANE, head(d)), device_id_type=MESH,
                        ).start()

            for d in heads:
                pltpu.make_async_remote_copy(
                    src_ref=st_wq.at[g, :, rows_at(head(d)), :], dst_ref=wq.at[:, :, out_cols(g)],
                    send_sem=wq_send.at[g], recv_sem=wq_recv,
                    device_id=(guest, head(d)), device_id_type=MESH,
                ).start()

    @pl.when(z == 0)
    def _():
        sum_over_plane()

    @pl.when(z == 0)
    def _():
        pl.semaphore_wait(line_sem.at[0], DEPTH - 1)
        for d in range(1, DEPTH):
            pl.semaphore_signal(line_sem.at[1], inc=1, device_id=(line(d), hd), device_id_type=MESH)

    @pl.when(z == 0)
    def _():
        sum_over_line()

    wait_for(landed.at[:, :, pl.ds(0, (NH - 1) * HG * W)], r_recv)
    for g in range(HG):
        wait_for(stage.at[g, :, pl.ds(0, ROWS)], own_sem)
    for s in (1, 2):

        @pl.when(ahead(s))
        def _():
            wait_for(back.at[s - 1], p_recv.at[s - 1])

        @pl.when(~behind(s))
        def _():
            wait_for(wkv.at[s - 1], pw_recv.at[s - 1])

    @pl.when(me < 2)
    def _():
        for i in range(2):
            first_term = jnp.where(me == 0, wkv[0, i].astype(F32), 0.0)
            total = landed[2 + 2 * i].astype(F32) + first_term + wkv[1, i].astype(F32)
            landed[2 + 2 * i] = total.astype(BF16)

    @pl.when(last_two)
    def _():
        wait_for(wq, wq_recv)
        landed[0] = (landed[0].astype(F32) + wq[0].astype(F32)).astype(BF16)
        back[1] = wq[1]


    for s in (1, 2):

        @pl.when(ahead(s))
        def _():
            wait_for(sent[0], qs_send.at[s - 1, 2])
            wait_for(nd, nd_send.at[s - 1])
            pass

        @pl.when(~behind(s))
        def _():
            wait_for(sent[1], ws_send.at[s - 1, 0])
            wait_for(sent[1], ws_send.at[s - 1, 1])
            pass

        @pl.when(behind(s))
        def _():
            wait_for(st_p.at[s - 1], p_send.at[s - 1])

        @pl.when(hosts(s))
        def _():
            for g in range(HG):
                wait_for(st_wkv.at[g, s - 1], pw_send.at[s - 1, g])


    @pl.when(relays)
    def _():
        wait_for(r_a.at[0, 1], f_send)

    @pl.when(host)
    def _():
        for g in range(HG):
            wait_for(st_wq.at[g], wq_send.at[g])
        pass

    @pl.when(last_two)
    def _():
        wait_for(q_v, hs_send.at[0])
        wait_for(q_v, hs_send.at[1])
        wait_for(nd, hs_send.at[2])
        pass

    for g in range(HG):
        wait_for(stage.at[g, :, pl.ds(0, (NH - 1) * ROWS)], r_send.at[g])
    wait_for(lbuf1.at[pl.ds(0, PLANE - 1)], l_send.at[0])
    wait_for(lbuf2.at[pl.ds(0, DEPTH - 1)], l_recv.at[1])
    wait_for(lbuf2.at[pl.ds(0, DEPTH - 1)], l_send.at[1])


def finish_kernel(landed, back, lbuf2, oq, ok, ov, lam_out, sum_q, sums, sems):
    copies = [
        pltpu.make_async_copy(landed.at[pl.ds(2, 2)], ok, sems.at[0]),
        pltpu.make_async_copy(landed.at[pl.ds(4, 2)], ov, sems.at[1]),
        pltpu.make_async_copy(landed.at[0], oq.at[0], sems.at[2]),
        pltpu.make_async_copy(sum_q, oq.at[1], sems.at[3]),
        pltpu.make_async_copy(sums, lam_out, sems.at[4]),
    ]
    for c in copies[:3]:
        c.start()
    sum_q[...] = (landed[1].astype(F32) + back[0].astype(F32) + back[1].astype(F32)).astype(BF16)
    copies[3].start()
    total = lbuf2[0]
    for i in range(1, DEPTH):
        total = total + lbuf2[i]
    for g in range(HG):
        sums[g] = -jnp.sum(total[g : g + 1, :])
    copies[4].start()
    for c in copies:
        c.wait()


def local(query_rows, key_rows, value_rows, out_grad, log_norms, row_deltas, lambdas):
    n = lax.axis_size("ctx")
    hbm = pl.BlockSpec(memory_space=pl.ANY)
    vmem = pl.BlockSpec(memory_space=pltpu.VMEM)
    half = (2, BLK, HG * W)
    dma, regular = pltpu.SemaphoreType.DMA, pltpu.SemaphoreType.REGULAR
    args = (
        query_rows, key_rows, value_rows, out_grad,
        jnp.swapaxes(log_norms, 1, 2), jnp.swapaxes(row_deltas, 1, 2), lambdas,
    )
    landed, back, sums = pl.pallas_call(
        functools.partial(main_kernel, n),
        out_shape=(
            pltpu.VMEM((6, ROWS, COLS), BF16), pltpu.VMEM((2, ROWS, COLS), BF16),
            pltpu.VMEM((DEPTH, 8, 128), F32),
        ),
        in_specs=[hbm] * 7,
        out_specs=(vmem,) * 3,
        scratch_shapes=[
            pltpu.SMEM((HG,), F32),
            pltpu.VMEM(half, BF16), pltpu.VMEM(half, BF16), pltpu.VMEM(half, BF16), pltpu.VMEM(half, BF16),
            pltpu.VMEM((2, HG, 2, BLK), F32), pltpu.VMEM((2, HG, 2, BLK), F32),
            pltpu.VMEM((16, 128), F32), pltpu.VMEM((16, 128), F32), pltpu.VMEM((2, 16, 128), F32),
            *[pltpu.VMEM((HG, 2, BLK, c), BF16) for c in (128 + W, 128, 2 * W, 2 * W)],
            pltpu.VMEM((16, 128), F32),
            *[pltpu.VMEM((HG, 2 * BLK, 2 * BLK), F32) for _ in range(2)],
            pltpu.VMEM((HG, 2, 2 * BLK, W), F32), pltpu.VMEM((HG, 6, BLK, W), BF16),
            pltpu.VMEM((2, BLK, HG * W), BF16),
            pltpu.VMEM((HG, 2, 2, BLK, W), BF16), pltpu.VMEM((HG, 2, BLK, W), BF16),
            pltpu.VMEM((2, 2, ROWS, COLS), BF16), pltpu.VMEM((2, ROWS, COLS), BF16),
            pltpu.VMEM((8, 128), F32), pltpu.VMEM((PLANE, 8, 128), F32),
            dma((7,)), dma, dma((2, 3)), dma((2, HG)), dma((2, HG)), dma, dma((2,)), dma((2,)),
            dma((2, 2)), dma((2, HG)), dma((3,)), dma((HG,)), dma, dma((HG,)), dma,
            dma((HG,)), dma, dma((2,)), dma((2,)), dma((2, HG)), dma((2,)), dma((2,)), dma((2,)),
            regular((3,)),
        ],
        compiler_params=pltpu.CompilerParams(
            collective_id=0, has_side_effects=True, vmem_limit_bytes=24 * 1024 * 1024
        ),
        cost_estimate=pl.CostEstimate(flops=3 * 10**8, bytes_accessed=2 * 10**6, transcendentals=2 * 10**5),
        name="attention_backward",
    )(*[pltpu.with_memory_space_constraint(x, pltpu.HBM) for x in args])
    out = jax.ShapeDtypeStruct((2, ROWS, COLS), BF16)
    return pl.pallas_call(
        finish_kernel,
        out_shape=(out, out, out, jax.ShapeDtypeStruct((HG,), F32)),
        in_specs=[vmem] * 3,
        out_specs=(hbm,) * 4,
        scratch_shapes=[pltpu.VMEM((ROWS, COLS), BF16), pltpu.SMEM((HG,), F32), dma((5,))],
        compiler_params=pltpu.CompilerParams(vmem_limit_bytes=16 * 1024 * 1024),
        name="write_outputs",
    )(*[pltpu.with_memory_space_constraint(x, pltpu.VMEM) for x in (landed, back, sums)])


def solution(mesh):
    in_specs = (
        P(None, "ctx", "head"),
        P(None, "ctx", "head"),
        P(None, "ctx", "head"),
        P(None, "ctx", "head"),
        P(None, None, "head", "ctx"),
        P(None, None, "head", "ctx"),
        P("head"),
    )
    out_specs = (
        P(None, ("ctx", "head"), None),
        P(None, ("ctx", "head"), None),
        P(None, ("ctx", "head"), None),
        P("head"),
    )
    return jax.shard_map(local, mesh=mesh, in_specs=in_specs, out_specs=out_specs, check_vma=False)
```
